128 devices in a mesh: snap: 16 (over y, z), ord: 8 (over x, core).
Axes of the slice: x: 4, y: 4, z: 4, core: 2. Of those that a mesh axis runs over, the one named last changes fastest.
Arguments:
- images: bfloat16 [2048, 256, 1024], P(('snap', 'ord')), may hold values from -8 to 8
- cycle_masks: int32 [2048, 256], P('snap'), may hold values from 0 to 1, as said below
- weights: float32 [2048], P('snap'), may hold values from 1 to 4
- inversion: float32 [128, 128], replicated, may hold values from -1 to 2
Outputs:
- kam: float32 [128, 256, 256], P('ord', 'snap')
The draws below stay inside these ranges and needn't reach their ends.
Inputs may be any that keep to these rules, and one draw needn't show every extreme that they name: `cycle_masks`: each entry is 0 or 1; the same 4 cycles, drawn from the seed, are 0 in every snapshot.
All inputs are finite; a program needn't handle non-finite values.
Results may differ from the reference program's by a relative error of at most 0.0015.
Values may be sent and summed in bfloat16 or wider, within the bound.
A program may use at most 64 MiB of HBM per device.

```python
import math
import jax
import jax.numpy as jnp
from jax import lax

CYCLES = 256
ANGLES = 1024
ORDERS = 128
DEAD_CYCLES = 4
SNAP_DEV = 16
SNAPSHOTS = 2048


def draw_images(key, part):
    cycle_gain = jax.random.uniform(jax.random.fold_in(key, 21), (1, CYCLES, 1), jnp.float32, 0.3, 1.0)
    noise = jax.random.normal(jax.random.fold_in(key, 29), (SNAPSHOTS, CYCLES, ANGLES), jnp.float32)
    common = jax.random.normal(jax.random.fold_in(key, 31), (SNAPSHOTS, 1, ANGLES), jnp.float32)
    values = 0.8 * noise + cycle_gain * common
    return jnp.clip(values, -8.0, 8.0).astype(jnp.bfloat16)


def draw_cycle_masks(key, part):
    threshold = jax.random.randint(jax.random.fold_in(key, 3), (SNAPSHOTS, 1), 300, 1001)
    alive_draw = jax.random.randint(jax.random.fold_in(key, 4), (SNAPSHOTS, CYCLES), 0, 1000) < threshold
    radius = jax.random.randint(jax.random.fold_in(key, 6), (SNAPSHOTS, 1), 0, CYCLES // 2)
    cycle_index = jnp.arange(CYCLES, dtype=jnp.int32)[None, :]
    outside = cycle_index >= radius
    cycle_rank = jax.random.permutation(jax.random.fold_in(key, 5), CYCLES)
    blocked = cycle_rank < DEAD_CYCLES
    alive = jnp.logical_and(alive_draw, outside).astype(jnp.int32)
    return jnp.where(blocked[None, :], 0, alive).astype(jnp.int32)


def draw_inversion(key, part):
    noise = jax.random.uniform(jax.random.fold_in(key, 7), (ORDERS, ORDERS), jnp.float32, -1.0, 1.0) * 0.6
    return jnp.eye(ORDERS, dtype=jnp.float32) + noise / jnp.sqrt(ORDERS * 1.0)


def shard_levels(key, dims, split, least, high):
    gain, own = 1.0, jax.random.fold_in(key, 6)
    for position, blocks in split:
        draws = jnp.exp(jax.random.uniform(jax.random.fold_in(own, position), (blocks,), jnp.float32, least / len(split), high / len(split)))
        gain = gain * jnp.repeat(draws, dims[position] // blocks).reshape([-1 if axis == position else 1 for axis in range(len(dims))])
    return gain


def setup_inputs(seed: int = 0) -> dict:
    keys = jax.random.split(jax.random.key(seed), 5)
    images = draw_images(jax.random.fold_in(keys[4], 71), 0)
    cycle_masks = draw_cycle_masks(jax.random.fold_in(keys[4], 71), 0)
    weights = jnp.clip(1.0 + 3.0 * jax.random.uniform(keys[2], (SNAPSHOTS,), jnp.float32) ** shard_levels(keys[2], (SNAPSHOTS,), ((0, 16),), -0.2, 0.2), 1.0, 4.0)
    inversion = draw_inversion(jax.random.fold_in(keys[4], 71), 0)
    return {"images": images, "cycle_masks": cycle_masks, "weights": weights, "inversion": inversion}


def make_table(orders, angles):
    order_index = jnp.arange(orders, dtype=jnp.int32)
    angle_index = jnp.arange(angles, dtype=jnp.int32)
    phase_index = order_index[:, None] * angle_index[None, :] % angles
    radians = phase_index.astype(jnp.float32) * (2.0 * math.pi / angles)
    norming = math.sqrt(2.0 / angles)
    return jnp.concatenate([jnp.cos(radians) * norming, -jnp.sin(radians) * norming], axis=0).astype(jnp.bfloat16)

def reference(images, cycle_masks, weights, inversion):
    dft_table = make_table(ORDERS, ANGLES)
    table_cols = dft_table.astype(jnp.float32).T
    block_count = images.shape[0] // SNAP_DEV

    def accumulate(state_pair, block_index):
        gram_sum, pair_count = state_pair
        first_row = (block_index * SNAP_DEV).astype(jnp.int32)
        image_block = lax.dynamic_slice_in_dim(images, first_row, SNAP_DEV, 0)
        mask_block = lax.dynamic_slice_in_dim(cycle_masks, first_row, SNAP_DEV, 0).astype(jnp.float32)
        weight_block = lax.dynamic_slice_in_dim(weights, first_row, SNAP_DEV, 0).astype(jnp.float32)
        flat_rows = image_block.reshape(SNAP_DEV * CYCLES, ANGLES).astype(jnp.float32)
        spectra = jnp.dot(flat_rows, table_cols, precision=lax.Precision.HIGHEST)
        coeffs = spectra.T.reshape(2 * ORDERS, SNAP_DEV, CYCLES)
        coeffs = (coeffs * mask_block[None]).astype(jnp.bfloat16).reshape(2, ORDERS, SNAP_DEV, CYCLES)
        weighted = (coeffs.astype(jnp.float32) * weight_block[None, None, :, None]).astype(jnp.bfloat16)
        gram_sum = gram_sum + jnp.einsum('rlsq,rlsp->lqp', weighted.astype(jnp.float32), coeffs.astype(jnp.float32), precision=lax.Precision.HIGHEST)
        masked_weight = mask_block * weight_block[:, None]
        pair_count = pair_count + jnp.einsum('sq,sp->qp', masked_weight, mask_block, precision=lax.Precision.HIGHEST)
        return ((gram_sum, pair_count), None)
    initial = (jnp.zeros((ORDERS, CYCLES, CYCLES), jnp.float32), jnp.zeros((CYCLES, CYCLES), jnp.float32))
    (gram_sum, pair_count), _ = lax.scan(accumulate, initial, jnp.arange(block_count, dtype=jnp.int32))
    correl = gram_sum / jnp.maximum(pair_count, 1.0)[None]
    kam = jnp.dot(inversion, correl.reshape(ORDERS, CYCLES * CYCLES), precision=lax.Precision.HIGHEST)
    return kam.reshape(ORDERS, CYCLES, CYCLES)
```

```python
import functools
import math

import jax
import jax.numpy as jnp
import numpy as np
from jax import lax
from jax.experimental import pallas as pl
from jax.experimental.pallas import tpu as pltpu
from jax.sharding import PartitionSpec as P

MESH = pl.DeviceIdType.MESH
SIDE = 4
GROUPS = SIDE * SIDE
LINE = 2 * SIDE
SNAPS = 16
CYCLES = 256
ANGLES = 1024
ORDERS = 128
HALF = ORDERS // 2


def make_table():
    order_index = np.arange(ORDERS)
    angle_index = np.arange(ANGLES)
    phase_index = order_index[:, None] * angle_index[None, :] % ANGLES
    radians = phase_index.astype(np.float32) * np.float32(2.0 * math.pi / ANGLES)
    norming = np.float32(math.sqrt(2.0 / ANGLES))
    table = np.concatenate([np.cos(radians) * norming, -np.sin(radians) * norming], axis=0)
    return table.astype(jnp.bfloat16)


def slot_offsets(slot):
    dy = slot % SIDE
    dz = (dy + slot // SIDE) % SIDE
    return dy, dz


def kernel(
    img_hbm, msk_hbm, wts_hbm, inv_hbm, tab_hbm, out_ref,
    img, tab, msk, wts, inv, spectra, coeffs, arrived, notes, notices, gram, tiles, kams,
    in_sems, img_sems, a_send, a_recv, n_send, n_recv, g_send, g_recv, h_send, h_recv, k_send, k_recv, ready,
):
    s = lax.axis_index("snap")
    o = lax.axis_index("ord")
    y, z = s // SIDE, s % SIDE
    x, c = o // 2, o % 2
    x_row, x_lane = x // 2, x % 2

    def group_at(dy, dz):
        return ((y + dy) % SIDE) * SIDE + (z + dz) % SIDE

    for k in range(SNAPS):
        pltpu.make_async_copy(img_hbm.at[k], img.at[k], img_sems.at[k]).start()
    small = [
        pltpu.make_async_copy(src, dst, in_sems.at[k])
        for k, (src, dst) in enumerate(
            [(tab_hbm, tab), (msk_hbm, msk), (wts_hbm, wts), (inv_hbm, inv)]
        )
    ]
    for copy in small:
        copy.start()

    barrier = pltpu.get_barrier_semaphore()

    def greet_line(k, carry):
        pl.semaphore_signal(barrier, inc=1, device_id=(s, (o + k) % LINE), device_id_type=MESH)
        return carry

    def greet_groups(k, carry):
        pl.semaphore_signal(barrier, inc=1, device_id=((s + k) % GROUPS, o), device_id_type=MESH)
        return carry

    lax.fori_loop(1, LINE, greet_line, 0)
    lax.fori_loop(1, GROUPS, greet_groups, 0)

    for copy in small[1:]:
        copy.wait()
    mask = msk[...].astype(jnp.float32)
    mask_half = msk[:, pl.ds(pl.multiple_of(x_lane * 128, 128), 128)].astype(jnp.float32)
    gram[:, 0:128] = jnp.dot(
        mask.T * wts[...], mask_half,
        precision=lax.Precision.HIGHEST, preferred_element_type=jnp.float32,
    )
    weight_rows = jnp.broadcast_to(wts[...], (8, 128))
    for k in range(GROUPS):
        notes[k, 0:8, :] = gram[pl.ds(pl.multiple_of(16 * k + 8 * x_row, 8), 8), 0:128]
        notes[k, 8:16, :] = weight_rows
    notices[0] = notes[s]

    pl.semaphore_wait(barrier, LINE - 1 + GROUPS - 1)

    def tell(k, carry):
        pl.semaphore_signal(ready, inc=1, device_id=((s + k) % GROUPS, o), device_id_type=MESH)
        return carry

    lax.fori_loop(1, GROUPS, tell, 0)

    def send_note(slot, carry):
        group = group_at(*slot_offsets(slot))
        pltpu.make_async_remote_copy(
            notes.at[group], notices.at[slot], n_send, n_recv, device_id=(group, o), device_id_type=MESH
        ).start()
        return carry

    lax.fori_loop(1, GROUPS, send_note, 0)

    small[0].wait()

    def transform(k, carry):
        pltpu.make_async_copy(img_hbm.at[k], img.at[k], img_sems.at[k]).wait()
        product = lax.dot_general(
            tab[...], img[k], (((1,), (1,)), ((), ())), preferred_element_type=jnp.float32
        )
        row = msk[pl.ds(o * SNAPS + k, 1), :].astype(jnp.float32)
        product = product * row
        place = pl.multiple_of(k * 2 * ORDERS, 2 * ORDERS)
        for lane in range(2):
            spectra[lane, pl.ds(place, 2 * ORDERS), :] = product[:, 128 * lane : 128 * lane + 128]
        return carry

    lax.fori_loop(0, SNAPS, transform, 0)

    pl.semaphore_wait(ready, GROUPS - 1)

    def gather(order):
        for part in range(2):
            for lane in range(2):
                rows = spectra[lane, pl.ds(part * ORDERS + order, SNAPS, stride=2 * ORDERS), :]
                coeffs[order, part, :, 128 * lane : 128 * lane + 128] = rows.astype(jnp.bfloat16)

    own_order = c * HALF + x * GROUPS + s
    gather(own_order)
    pltpu.make_async_copy(coeffs.at[own_order], arrived.at[0, :, o], a_recv.at[0]).start()

    def send_coeffs(i, carry):
        wave, step = i // 32, i % 32
        dy = step % 4
        dz = (dy + wave) % 4
        dx = (step // 4) % 4
        dc = step // 16
        group = group_at(dy, dz)
        there_x, there_c = (x + dx) % SIDE, (c + dc) % 2
        order = there_c * HALF + there_x * GROUPS + group
        gather(order)
        slot = wave * 4 + dy
        pltpu.make_async_remote_copy(
            coeffs.at[order], arrived.at[slot, :, o], a_send, a_recv.at[slot],
            device_id=(group, there_x * 2 + there_c), device_id_type=MESH,
        ).start()
        return carry

    lax.fori_loop(1, ORDERS, send_coeffs, 0)

    pltpu.make_async_copy(notices.at[pl.ds(1, 15)], notices.at[pl.ds(1, 15)], n_recv).wait()
    gram[...] = jnp.zeros_like(gram)

    def add_group(slot, carry):
        pltpu.make_async_copy(arrived.at[slot], arrived.at[slot], a_recv.at[slot]).wait()
        block = arrived[slot].reshape(2 * LINE * SNAPS, CYCLES)
        weight = notices[slot, 8:9, :]
        weight = jnp.concatenate([weight, weight], axis=1)
        weighted = (block.astype(jnp.float32).T * weight).astype(jnp.bfloat16)
        gram[...] += jnp.dot(weighted, block, preferred_element_type=jnp.float32)
        return carry

    lax.fori_loop(0, GROUPS, add_group, 0)

    tile_rows = pl.ds(pl.multiple_of(8 * own_order, 8), 8)

    def gram_tile(group, chip):
        row = pl.multiple_of(16 * group + 8 * (chip // 2), 8)
        lane = pl.multiple_of(128 * (chip % 2), 128)
        return gram.at[pl.ds(row, 8), pl.ds(lane, 128)]

    pltpu.make_async_copy(gram_tile(s, x), tiles.at[tile_rows], g_recv).start()

    def send_tile(i, carry):
        wave, step = i // 16, i % 16
        dy = step % 4
        dz = (dy + wave) % 4
        dx = step // 4
        group = group_at(dy, dz)
        there_x = (x + dx) % SIDE
        pltpu.make_async_remote_copy(
            gram_tile(group, there_x), tiles.at[tile_rows], g_send, g_recv,
            device_id=(group, there_x * 2 + c), device_id_type=MESH,
        ).start()
        return carry

    lax.fori_loop(1, HALF, send_tile, 0)

    own_half = tiles.at[pl.ds(pl.multiple_of(8 * HALF * c, 8 * HALF), 8 * HALF)]
    pltpu.make_async_copy(own_half, own_half, g_recv).wait()
    swap = pltpu.make_async_remote_copy(
        own_half, own_half, h_send, h_recv, device_id=(s, x * 2 + 1 - c), device_id_type=MESH
    )
    swap.start()
    count = notices[0, 0:8, :]
    for k in range(1, GROUPS):
        count += notices[k, 0:8, :]
    count = jnp.maximum(count, 1.0)
    own_inv = jnp.concatenate(
        [inv[pl.ds(pl.multiple_of(32 * k + 16 * c, 16), 16), :] for k in range(SIDE)], axis=0
    )
    swap.wait()

    flat_kams = kams.reshape(HALF * 8, 128)
    for r in range(8):
        grams = tiles[pl.ds(r, ORDERS, stride=8), :]
        correl = grams / count[r : r + 1, :]
        flat_kams[pl.ds(r, HALF, stride=8), :] = jnp.dot(
            own_inv, correl, precision=lax.Precision.HIGHEST, preferred_element_type=jnp.float32
        )

    place = out_ref.at[:, pl.ds(pl.multiple_of(8 * x_row, 8), 8), pl.ds(pl.multiple_of(128 * x_lane, 128), 128)]
    for d in range(1, SIDE):
        there_x = (x + d) % SIDE
        pltpu.make_async_remote_copy(
            kams.at[pl.ds(16 * there_x, 16)], place, k_send, k_recv,
            device_id=(s, there_x * 2 + c), device_id_type=MESH,
        ).start()
    pltpu.make_async_copy(kams.at[pl.ds(16 * x, 16)], place, k_recv).start()

    pltpu.make_async_copy(notes.at[pl.ds(0, 15)], notes.at[pl.ds(0, 15)], n_send).wait()
    pltpu.make_async_copy(coeffs.at[pl.ds(0, 127)], coeffs.at[pl.ds(0, 127)], a_send).wait()
    pltpu.make_async_copy(tiles.at[pl.ds(0, 504)], tiles.at[pl.ds(0, 504)], g_send).wait()
    pltpu.make_async_copy(kams.at[pl.ds(0, 48)], kams.at[pl.ds(0, 48)], k_send).wait()
    pltpu.make_async_copy(out_ref, out_ref, k_recv).wait()


def on_device(images, cycle_masks, weights, inversion):
    hbm = pl.BlockSpec(memory_space=pl.ANY)
    dma, regular = pltpu.SemaphoreType.DMA, pltpu.SemaphoreType.REGULAR
    f32, bf16 = jnp.float32, jnp.bfloat16
    return pl.pallas_call(
        kernel,
        out_shape=jax.ShapeDtypeStruct((16, 16, CYCLES), f32),
        in_specs=[hbm] * 5,
        out_specs=hbm,
        scratch_shapes=[
            pltpu.VMEM((SNAPS, CYCLES, ANGLES), bf16),
            pltpu.VMEM((2 * ORDERS, ANGLES), bf16),
            pltpu.VMEM((LINE * SNAPS, CYCLES), jnp.int32),
            pltpu.VMEM((1, LINE * SNAPS), f32),
            pltpu.VMEM((ORDERS, ORDERS), f32),
            pltpu.VMEM((2, SNAPS * 2 * ORDERS, 128), f32),
            pltpu.VMEM((ORDERS, 2, SNAPS, CYCLES), bf16),
            pltpu.VMEM((GROUPS, 2, LINE, SNAPS, CYCLES), bf16),
            pltpu.VMEM((GROUPS, 16, 128), f32),
            pltpu.VMEM((GROUPS, 16, 128), f32),
            pltpu.VMEM((CYCLES, CYCLES), f32),
            pltpu.VMEM((ORDERS * 8, 128), f32),
            pltpu.VMEM((HALF, 8, 128), f32),
            dma((4,)),
            dma((SNAPS,)),
            dma,
            dma((GROUPS,)),
            dma, dma, dma, dma, dma, dma, dma, dma,
            regular,
        ],
        compiler_params=pltpu.CompilerParams(
            collective_id=0, has_side_effects=True, vmem_limit_bytes=48 * 2**20
        ),
        name="kam",
    )(images, cycle_masks, weights.reshape(1, -1), inversion, jnp.asarray(make_table()))


def solution(mesh):
    placed = (P(("snap", "ord"), None, None), P("snap", None), P("snap"), P())
    return jax.shard_map(
        on_device, mesh=mesh, in_specs=placed, out_specs=P("ord", "snap", None), check_vma=False
    )
```

```python
import functools
import math

import jax
import jax.numpy as jnp
import numpy as np
from jax import lax
from jax.experimental import pallas as pl
from jax.experimental.pallas import tpu as pltpu
from jax.sharding import PartitionSpec as P

MESH = pl.DeviceIdType.MESH
SIDE = 4
GROUPS = SIDE * SIDE
LINE = 2 * SIDE
SNAPS = 16
CYCLES = 256
ANGLES = 1024
ORDERS = 128
HALF = ORDERS // 2
CHUNK = 4


def make_table():
    order_index = np.arange(ORDERS)
    angle_index = np.arange(ANGLES)
    phase_index = order_index[:, None] * angle_index[None, :] % ANGLES
    radians = phase_index.astype(np.float32) * np.float32(2.0 * math.pi / ANGLES)
    norming = np.float32(math.sqrt(2.0 / ANGLES))
    table = np.concatenate([np.cos(radians) * norming, -np.sin(radians) * norming], axis=0)
    return table.astype(jnp.bfloat16)


def slot_offsets(slot):
    dy = slot % SIDE
    dz = (dy + slot // SIDE) % SIDE
    return dy, dz


def farthest_first(k):
    return jnp.where(k == 3, 0, jnp.where(k == 2, 3, 2 - k))


def kernel(
    img_hbm, msk_hbm, wts_hbm, inv_hbm, tab_hbm, out_ref,
    img, tab, msk, wts, inv, spectra, coeffs, arrived, notes, notices, gram, tiles, kams,
    in_sems, img_sems, a_send, a_recv, n_send, n_recv, g_send, g_recv, h_send, h_recv, k_send, k_recv, ready,
):
    s = lax.axis_index("snap")
    o = lax.axis_index("ord")
    y, z = s // SIDE, s % SIDE
    x, c = o // 2, o % 2
    x_row, x_lane = x // 2, x % 2

    def group_at(dy, dz):
        return ((y + dy) % SIDE) * SIDE + (z + dz) % SIDE

    small = [
        pltpu.make_async_copy(src, dst, in_sems.at[k])
        for k, (src, dst) in enumerate(
            [(tab_hbm, tab), (msk_hbm, msk), (wts_hbm, wts), (inv_hbm, inv)]
        )
    ]
    small[0].start()
    for k in range(SNAPS // CHUNK):
        part = pl.ds(k * CHUNK, CHUNK)
        pltpu.make_async_copy(img_hbm.at[part], img.at[part], img_sems.at[k]).start()
        if k == 0:
            for copy in small[1:]:
                copy.start()

    barrier = pltpu.get_barrier_semaphore()

    def greet_line(k, carry):
        pl.semaphore_signal(barrier, inc=1, device_id=(s, (o + k) % LINE), device_id_type=MESH)
        return carry

    def greet_groups(k, carry):
        pl.semaphore_signal(barrier, inc=1, device_id=((s + k) % GROUPS, o), device_id_type=MESH)
        return carry

    lax.fori_loop(1, LINE, greet_line, 0)
    lax.fori_loop(1, GROUPS, greet_groups, 0)

    for copy in small[1:]:
        copy.wait()
    mask = msk[...].astype(jnp.float32)
    mask_half = msk[:, pl.ds(pl.multiple_of(x_lane * 128, 128), 128)].astype(jnp.float32)
    gram[:, 0:128] = jnp.dot(
        mask.T * wts[...], mask_half,
        precision=lax.Precision.HIGHEST, preferred_element_type=jnp.float32,
    )
    weight_rows = jnp.broadcast_to(wts[...], (8, 128))
    for k in range(GROUPS):
        notes[k, 0:8, :] = gram[pl.ds(pl.multiple_of(16 * k + 8 * x_row, 8), 8), 0:128]
        notes[k, 8:16, :] = weight_rows
    notices[0] = notes[s]

    pl.semaphore_wait(barrier, LINE - 1 + GROUPS - 1)

    def tell(k, carry):
        pl.semaphore_signal(ready, inc=1, device_id=((s + k) % GROUPS, o), device_id_type=MESH)
        return carry

    lax.fori_loop(1, GROUPS, tell, 0)

    def send_note(slot, carry):
        group = group_at(*slot_offsets(slot))
        pltpu.make_async_remote_copy(
            notes.at[group], notices.at[slot], n_send, n_recv, device_id=(group, o), device_id_type=MESH
        ).start()
        return carry

    lax.fori_loop(1, GROUPS, send_note, 0)

    small[0].wait()

    def transform(chunk, carry):
        first = chunk * CHUNK
        loads = img.at[pl.ds(first, CHUNK)]
        pltpu.make_async_copy(loads, loads, img_sems.at[chunk]).wait()
        for u in range(CHUNK):
            k = first + u
            product = lax.dot_general(
                tab[...], img[k], (((1,), (1,)), ((), ())), preferred_element_type=jnp.float32
            )
            product = product * msk[pl.ds(o * SNAPS + k, 1), :].astype(jnp.float32)
            place = pl.multiple_of(k * 2 * ORDERS, 2 * ORDERS)
            for lane in range(2):
                spectra[lane, pl.ds(place, 2 * ORDERS), :] = product[:, 128 * lane : 128 * lane + 128]
        return carry

    lax.fori_loop(0, SNAPS // CHUNK, transform, 0)

    pl.semaphore_wait(ready, GROUPS - 1)

    def gather(order):
        for part in range(2):
            for lane in range(2):
                rows = spectra[lane, pl.ds(part * ORDERS + order, SNAPS, stride=2 * ORDERS), :]
                coeffs[order, part, :, 128 * lane : 128 * lane + 128] = rows.astype(jnp.bfloat16)

    own_order = c * HALF + x * GROUPS + s
    gather(own_order)
    pltpu.make_async_copy(coeffs.at[own_order], arrived.at[0, :, o], a_recv.at[0]).start()

    def send_coeffs(i, carry):
        wave, step = i // 32, i % 32
        dy = step % 4
        dz = (dy + wave) % 4
        dx = (step // 4) % 4
        dc = step // 16
        group = group_at(dy, dz)
        there_x, there_c = (x + dx) % SIDE, (c + dc) % 2
        order = there_c * HALF + there_x * GROUPS + group
        gather(order)
        slot = wave * 4 + dy
        pltpu.make_async_remote_copy(
            coeffs.at[order], arrived.at[slot, :, o], a_send, a_recv.at[slot],
            device_id=(group, there_x * 2 + there_c), device_id_type=MESH,
        ).start()
        return carry

    lax.fori_loop(1, ORDERS, send_coeffs, 0)

    pltpu.make_async_copy(notices.at[pl.ds(1, 15)], notices.at[pl.ds(1, 15)], n_recv).wait()
    gram[...] = jnp.zeros_like(gram)

    def add_group(slot, carry):
        pltpu.make_async_copy(arrived.at[slot], arrived.at[slot], a_recv.at[slot]).wait()
        block = arrived[slot].reshape(2 * LINE * SNAPS, CYCLES)
        weight = notices[slot, 8:9, :]
        weight = jnp.concatenate([weight, weight], axis=1)
        weighted = (block.astype(jnp.float32).T * weight).astype(jnp.bfloat16)
        gram[...] += jnp.dot(weighted, block, preferred_element_type=jnp.float32)
        return carry

    lax.fori_loop(0, GROUPS, add_group, 0)

    tile_rows = pl.ds(pl.multiple_of(8 * own_order, 8), 8)

    def gram_tile(group, chip):
        row = pl.multiple_of(16 * group + 8 * (chip // 2), 8)
        lane = pl.multiple_of(128 * (chip % 2), 128)
        return gram.at[pl.ds(row, 8), pl.ds(lane, 128)]

    pltpu.make_async_copy(gram_tile(s, x), tiles.at[tile_rows], g_recv.at[0]).start()

    def send_tile(i, carry):
        wave, step = i // 16, i % 16
        dx = farthest_first(wave)
        dy = farthest_first(step % 4)
        dz = farthest_first(step // 4)
        group = group_at(dy, dz)
        there_x = (x + dx) % SIDE

        @pl.when(i < HALF - 1)
        def _():
            pltpu.make_async_remote_copy(
                gram_tile(group, there_x), tiles.at[tile_rows], g_send, g_recv.at[dx],
                device_id=(group, there_x * 2 + c), device_id_type=MESH,
            ).start()

        return carry

    lax.fori_loop(0, HALF, send_tile, 0)

    for wave in range(SIDE):
        dx = (2, 1, 3, 0)[wave]
        row = pl.multiple_of(8 * (c * HALF + ((x + SIDE - dx) % SIDE) * GROUPS), 8 * GROUPS)
        part = tiles.at[pl.ds(row, 8 * GROUPS)]
        pltpu.make_async_copy(part, part, g_recv.at[dx]).wait()
        swap = pltpu.make_async_remote_copy(
            part, part, h_send, h_recv, device_id=(s, x * 2 + 1 - c), device_id_type=MESH
        )
        swap.start()
    count = notices[0, 0:8, :]
    for k in range(1, GROUPS):
        count += notices[k, 0:8, :]
    count = jnp.maximum(count, 1.0)
    own_inv = jnp.concatenate(
        [inv[pl.ds(pl.multiple_of(32 * k + 16 * c, 16), 16), :] for k in range(SIDE)], axis=0
    )
    own_half = tiles.at[pl.ds(pl.multiple_of(8 * HALF * c, 8 * HALF), 8 * HALF)]
    other_half = tiles.at[pl.ds(pl.multiple_of(8 * HALF * (1 - c), 8 * HALF), 8 * HALF)]
    pltpu.make_async_copy(own_half, own_half, h_send).wait()
    pltpu.make_async_copy(other_half, other_half, h_recv).wait()

    flat_kams = kams.reshape(HALF * 8, 128)
    for r in range(8):
        grams = tiles[pl.ds(r, ORDERS, stride=8), :]
        correl = grams / count[r : r + 1, :]
        flat_kams[pl.ds(r, HALF, stride=8), :] = jnp.dot(
            own_inv, correl, precision=lax.Precision.HIGHEST, preferred_element_type=jnp.float32
        )

    place = out_ref.at[:, pl.ds(pl.multiple_of(8 * x_row, 8), 8), pl.ds(pl.multiple_of(128 * x_lane, 128), 128)]
    for d in range(1, SIDE):
        there_x = (x + d) % SIDE
        pltpu.make_async_remote_copy(
            kams.at[pl.ds(16 * there_x, 16)], place, k_send, k_recv,
            device_id=(s, there_x * 2 + c), device_id_type=MESH,
        ).start()
    pltpu.make_async_copy(kams.at[pl.ds(16 * x, 16)], place, k_recv).start()

    pltpu.make_async_copy(notes.at[pl.ds(0, 15)], notes.at[pl.ds(0, 15)], n_send).wait()
    pltpu.make_async_copy(coeffs.at[pl.ds(0, 127)], coeffs.at[pl.ds(0, 127)], a_send).wait()
    pltpu.make_async_copy(tiles.at[pl.ds(0, 504)], tiles.at[pl.ds(0, 504)], g_send).wait()
    pltpu.make_async_copy(kams.at[pl.ds(0, 48)], kams.at[pl.ds(0, 48)], k_send).wait()
    pltpu.make_async_copy(out_ref, out_ref, k_recv).wait()


def on_device(images, cycle_masks, weights, inversion):
    operands = (images, cycle_masks, weights.reshape(1, -1), inversion, jnp.asarray(make_table()))
    dma, regular = pltpu.SemaphoreType.DMA, pltpu.SemaphoreType.REGULAR
    f32, bf16 = jnp.float32, jnp.bfloat16
    return pl.pallas_call(
        kernel,
        out_shape=pltpu.VMEM((16, 16, CYCLES), f32),
        in_specs=[pl.BlockSpec(memory_space=pltpu.HBM)] * 5,
        out_specs=pl.BlockSpec(memory_space=pltpu.VMEM),
        scratch_shapes=[
            pltpu.VMEM((SNAPS, CYCLES, ANGLES), bf16),
            pltpu.VMEM((2 * ORDERS, ANGLES), bf16),
            pltpu.VMEM((LINE * SNAPS, CYCLES), jnp.int32),
            pltpu.VMEM((1, LINE * SNAPS), f32),
            pltpu.VMEM((ORDERS, ORDERS), f32),
            pltpu.VMEM((2, SNAPS * 2 * ORDERS, 128), f32),
            pltpu.VMEM((ORDERS, 2, SNAPS, CYCLES), bf16),
            pltpu.VMEM((GROUPS, 2, LINE, SNAPS, CYCLES), bf16),
            pltpu.VMEM((GROUPS, 16, 128), f32),
            pltpu.VMEM((GROUPS, 16, 128), f32),
            pltpu.VMEM((CYCLES, CYCLES), f32),
            pltpu.VMEM((ORDERS * 8, 128), f32),
            pltpu.VMEM((HALF, 8, 128), f32),
            dma((4,)),
            dma((SNAPS // CHUNK,)),
            dma,
            dma((GROUPS,)),
            dma, dma, dma,
            dma((SIDE,)),
            dma, dma, dma, dma,
            regular,
        ],
        compiler_params=pltpu.CompilerParams(
            collective_id=0, has_side_effects=True, vmem_limit_bytes=48 * 2**20
        ),
        name="kam",
    )(*(pltpu.with_memory_space_constraint(value, pltpu.HBM) for value in operands))


def solution(mesh):
    placed = (P(("snap", "ord"), None, None), P("snap", None), P("snap"), P())
    return jax.shard_map(
        on_device, mesh=mesh, in_specs=placed, out_specs=P("ord", "snap", None), check_vma=False
    )
```

```python
import functools
import math

import jax
import jax.numpy as jnp
import numpy as np
from jax import lax
from jax.experimental import pallas as pl
from jax.experimental.pallas import tpu as pltpu
from jax.sharding import PartitionSpec as P

MESH = pl.DeviceIdType.MESH
SIDE = 4
GROUPS = SIDE * SIDE
LINE = 2 * SIDE
SNAPS = 16
CYCLES = 256
ANGLES = 1024
ORDERS = 128
HALF = ORDERS // 2
CHUNK = 4


def make_table():
    order_index = np.arange(ORDERS)
    angle_index = np.arange(ANGLES)
    phase_index = order_index[:, None] * angle_index[None, :] % ANGLES
    radians = phase_index.astype(np.float32) * np.float32(2.0 * math.pi / ANGLES)
    norming = np.float32(math.sqrt(2.0 / ANGLES))
    table = np.concatenate([np.cos(radians) * norming, -np.sin(radians) * norming], axis=0)
    return table.astype(jnp.bfloat16)


HOPS = sorted(
    [(hx, hy, hz) for hx in (2, 1, 0) for hy in (2, 1, 0) for hz in (2, 1, 0)], key=lambda hops: -sum(hops)
)


def for_each_offset(visit, cores=2, lines=True):
    for hops in HOPS:
        if not lines and hops[0]:
            continue
        first = 1 if sum(hops) == 0 else 0
        last = cores * 2 ** sum(h == 1 for h in hops)

        def step(k, carry, hops=hops):
            dc = k % cores
            signs = k // cores
            offsets = []
            for h in hops:
                if h == 1:
                    offsets.append(1 + 2 * (signs % 2))
                    signs = signs // 2
                else:
                    offsets.append(h)
            visit(offsets[0], dc, offsets[1], offsets[2])
            return carry

        if first < last:
            lax.fori_loop(first, last, step, 0)


SLOTS = sorted(
    [(dy, dz) for dy in range(SIDE) for dz in range(SIDE)],
    key=lambda offset: -sum(min(d, SIDE - d) for d in offset),
)


def kernel(
    img_hbm, msk_hbm, wts_hbm, inv_hbm, tab_hbm, out_ref,
    img, tab, msk, wts, inv, spectra, coeffs, arrived, counts, all_counts, all_wts, gram, tiles, kams,
    in_sems, img_sems, w_send, w_recv, a_send, a_recv, n_send, n_recv, g_send, g_recv, h_send, h_recv, k_send, k_recv,
):
    s = lax.axis_index("snap")
    o = lax.axis_index("ord")
    y, z = s // SIDE, s % SIDE
    x, c = o // 2, o % 2
    x_row, x_lane = x // 2, x % 2

    small = [
        pltpu.make_async_copy(src, dst, in_sems.at[k])
        for k, (src, dst) in enumerate(
            [(tab_hbm, tab), (msk_hbm, msk), (wts_hbm, wts), (inv_hbm, inv)]
        )
    ]
    small[0].start()
    for k in range(SNAPS // CHUNK):
        part = pl.ds(k * CHUNK, CHUNK)
        pltpu.make_async_copy(img_hbm.at[part], img.at[part], img_sems.at[k]).start()
        if k == 0:
            for copy in small[1:]:
                copy.start()

    barrier = pltpu.get_barrier_semaphore()

    def there(dx, dc, dy, dz):
        return ((y + dy) % SIDE) * SIDE + (z + dz) % SIDE, ((x + dx) % SIDE) * 2 + (c + dc) % 2

    def greet(*offset):
        pl.semaphore_signal(barrier, inc=1, device_id=there(*offset), device_id_type=MESH)

    for_each_offset(greet)

    for copy in small[1:]:
        copy.wait()
    mask = msk[...].astype(jnp.float32)
    mask_half = msk[:, pl.ds(pl.multiple_of(x_lane * 128, 128), 128)].astype(jnp.float32)
    counts[...] = jnp.dot(
        mask.T * wts[...], mask_half,
        precision=lax.Precision.HIGHEST, preferred_element_type=jnp.float32,
    )

    def count_tile(group):
        return counts.at[pl.ds(pl.multiple_of(16 * group + 8 * x_row, 8), 8), :]

    small[0].wait()

    def transform(chunk, carry):
        first = chunk * CHUNK
        loads = img.at[pl.ds(first, CHUNK)]
        pltpu.make_async_copy(loads, loads, img_sems.at[chunk]).wait()
        for u in range(CHUNK):
            k = first + u
            product = lax.dot_general(
                tab[...], img[k], (((1,), (1,)), ((), ())), preferred_element_type=jnp.float32
            )
            product = product * msk[pl.ds(o * SNAPS + k, 1), :].astype(jnp.float32)
            place = pl.multiple_of(k * 2 * ORDERS, 2 * ORDERS)
            for lane in range(2):
                spectra[lane, pl.ds(place, 2 * ORDERS), :] = product[:, 128 * lane : 128 * lane + 128]
        return carry

    lax.fori_loop(0, SNAPS // CHUNK, transform, 0)

    pl.semaphore_wait(barrier, GROUPS * LINE - 1)

    def send_weights(dx, dc, dy, dz):
        group, _ = there(0, 0, dy, dz)
        pltpu.make_async_remote_copy(
            wts, all_wts.at[SIDE * dy + dz], w_send, w_recv, device_id=(group, o), device_id_type=MESH
        ).start()

    for_each_offset(send_weights, cores=1, lines=False)
    all_wts[0] = wts[...]

    def gather(order):
        for part in range(2):
            for lane in range(2):
                rows = spectra[lane, pl.ds(part * ORDERS + order, SNAPS, stride=2 * ORDERS), :]
                coeffs[order, part, :, 128 * lane : 128 * lane + 128] = rows.astype(jnp.bfloat16)

    own_order = c * HALF + x * GROUPS + s
    gather(own_order)
    pltpu.make_async_copy(coeffs.at[own_order], arrived.at[0, :, o], a_recv.at[0]).start()

    def send_coeffs(*offset):
        group, line = there(*offset)
        order = (line % 2) * HALF + (line // 2) * GROUPS + group
        gather(order)
        slot = SIDE * offset[2] + offset[3]
        pltpu.make_async_remote_copy(
            coeffs.at[order], arrived.at[slot, :, o], a_send, a_recv.at[slot],
            device_id=(group, line), device_id_type=MESH,
        ).start()

    for_each_offset(send_coeffs)

    pltpu.make_async_copy(all_wts.at[pl.ds(1, 15)], all_wts.at[pl.ds(1, 15)], w_recv).wait()
    gram[...] = jnp.zeros_like(gram)

    for dy, dz in SLOTS:
        slot = SIDE * dy + dz
        pltpu.make_async_copy(arrived.at[slot], arrived.at[slot], a_recv.at[slot]).wait()
        block = arrived[slot].reshape(2 * LINE * SNAPS, CYCLES)
        weight = jnp.concatenate([all_wts[slot], all_wts[slot]], axis=1)
        weighted = (block.astype(jnp.float32).T * weight).astype(jnp.bfloat16)
        gram[...] += jnp.dot(weighted, block, preferred_element_type=jnp.float32)

    tile_rows = pl.ds(pl.multiple_of(8 * own_order, 8), 8)

    def gram_tile(group, chip):
        row = pl.multiple_of(16 * group + 8 * (chip // 2), 8)
        lane = pl.multiple_of(128 * (chip % 2), 128)
        return gram.at[pl.ds(row, 8), pl.ds(lane, 128)]

    pltpu.make_async_copy(gram_tile(s, x), tiles.at[tile_rows], g_recv.at[0]).start()

    def send_tile(dx, dc, dy, dz):
        group, line = there(dx, 0, dy, dz)
        pltpu.make_async_remote_copy(
            gram_tile(group, line // 2), tiles.at[tile_rows], g_send, g_recv.at[dx],
            device_id=(group, line), device_id_type=MESH,
        ).start()

    for_each_offset(send_tile, cores=1)

    def send_count(dx, dc, dy, dz):
        group, _ = there(0, 0, dy, dz)
        pltpu.make_async_remote_copy(
            count_tile(group), all_counts.at[SIDE * dy + dz], n_send, n_recv,
            device_id=(group, o), device_id_type=MESH,
        ).start()

    for_each_offset(send_count, cores=1, lines=False)
    pltpu.make_async_copy(count_tile(s), all_counts.at[0], n_recv).start()

    for wave in range(SIDE):
        dx = (2, 1, 3, 0)[wave]
        row = pl.multiple_of(8 * (c * HALF + ((x + SIDE - dx) % SIDE) * GROUPS), 8 * GROUPS)
        part = tiles.at[pl.ds(row, 8 * GROUPS)]
        pltpu.make_async_copy(part, part, g_recv.at[dx]).wait()
        swap = pltpu.make_async_remote_copy(
            part, part, h_send, h_recv, device_id=(s, x * 2 + 1 - c), device_id_type=MESH
        )
        swap.start()
    own_inv = jnp.concatenate(
        [inv[pl.ds(pl.multiple_of(32 * k + 16 * c, 16), 16), :] for k in range(SIDE)], axis=0
    )
    own_half = tiles.at[pl.ds(pl.multiple_of(8 * HALF * c, 8 * HALF), 8 * HALF)]
    other_half = tiles.at[pl.ds(pl.multiple_of(8 * HALF * (1 - c), 8 * HALF), 8 * HALF)]
    pltpu.make_async_copy(own_half, own_half, h_send).wait()
    pltpu.make_async_copy(other_half, other_half, h_recv).wait()

    pltpu.make_async_copy(all_counts, all_counts, n_recv).wait()
    count = jnp.maximum(jnp.sum(all_counts[...], axis=0), 1.0)

    flat_kams = kams.reshape(HALF * 8, 128)
    for r in range(8):
        grams = tiles[pl.ds(r, ORDERS, stride=8), :]
        correl = grams / count[r : r + 1, :]
        flat_kams[pl.ds(r, HALF, stride=8), :] = jnp.dot(
            own_inv, correl, precision=lax.Precision.HIGHEST, preferred_element_type=jnp.float32
        )

    place = out_ref.at[:, pl.ds(pl.multiple_of(8 * x_row, 8), 8), pl.ds(pl.multiple_of(128 * x_lane, 128), 128)]
    for d in (2, 1, 3):
        there_x = (x + d) % SIDE
        pltpu.make_async_remote_copy(
            kams.at[pl.ds(16 * there_x, 16)], place, k_send, k_recv,
            device_id=(s, there_x * 2 + c), device_id_type=MESH,
        ).start()
    pltpu.make_async_copy(kams.at[pl.ds(16 * x, 16)], place, k_recv).start()

    pltpu.make_async_copy(all_wts.at[pl.ds(0, 15)], all_wts.at[pl.ds(0, 15)], w_send).wait()
    pltpu.make_async_copy(all_counts.at[pl.ds(0, 15)], all_counts.at[pl.ds(0, 15)], n_send).wait()
    pltpu.make_async_copy(coeffs.at[pl.ds(0, 127)], coeffs.at[pl.ds(0, 127)], a_send).wait()
    pltpu.make_async_copy(tiles.at[pl.ds(0, 504)], tiles.at[pl.ds(0, 504)], g_send).wait()
    pltpu.make_async_copy(kams.at[pl.ds(0, 48)], kams.at[pl.ds(0, 48)], k_send).wait()
    pltpu.make_async_copy(out_ref, out_ref, k_recv).wait()


def on_device(images, cycle_masks, weights, inversion):
    operands = (images, cycle_masks, weights.reshape(1, -1), inversion, jnp.asarray(make_table()))
    dma = pltpu.SemaphoreType.DMA
    f32, bf16 = jnp.float32, jnp.bfloat16
    return pl.pallas_call(
        kernel,
        out_shape=pltpu.VMEM((16, 16, CYCLES), f32),
        in_specs=[pl.BlockSpec(memory_space=pltpu.HBM)] * 5,
        out_specs=pl.BlockSpec(memory_space=pltpu.VMEM),
        scratch_shapes=[
            pltpu.VMEM((SNAPS, CYCLES, ANGLES), bf16),
            pltpu.VMEM((2 * ORDERS, ANGLES), bf16),
            pltpu.VMEM((LINE * SNAPS, CYCLES), jnp.int32),
            pltpu.VMEM((1, LINE * SNAPS), f32),
            pltpu.VMEM((ORDERS, ORDERS), f32),
            pltpu.VMEM((2, SNAPS * 2 * ORDERS, 128), f32),
            pltpu.VMEM((ORDERS, 2, SNAPS, CYCLES), bf16),
            pltpu.VMEM((GROUPS, 2, LINE, SNAPS, CYCLES), bf16),
            pltpu.VMEM((CYCLES, 128), f32),
            pltpu.VMEM((GROUPS, 8, 128), f32),
            pltpu.VMEM((GROUPS, 1, LINE * SNAPS), f32),
            pltpu.VMEM((CYCLES, CYCLES), f32),
            pltpu.VMEM((ORDERS * 8, 128), f32),
            pltpu.VMEM((HALF, 8, 128), f32),
            dma((4,)),
            dma((SNAPS // CHUNK,)),
            dma, dma, dma,
            dma((GROUPS,)),
            dma, dma, dma,
            dma((SIDE,)),
            dma, dma, dma, dma,
        ],
        compiler_params=pltpu.CompilerParams(
            collective_id=0, has_side_effects=True, vmem_limit_bytes=48 * 2**20
        ),
        name="kam",
    )(*(pltpu.with_memory_space_constraint(value, pltpu.HBM) for value in operands))


def solution(mesh):
    placed = (P(("snap", "ord"), None, None), P("snap", None), P("snap"), P())
    return jax.shard_map(
        on_device, mesh=mesh, in_specs=placed, out_specs=P("ord", "snap", None), check_vma=False
    )
```

```python
import functools
import math

import jax
import jax.numpy as jnp
import numpy as np
from jax import lax
from jax.experimental import pallas as pl
from jax.experimental.pallas import tpu as pltpu
from jax.sharding import PartitionSpec as P

MESH = pl.DeviceIdType.MESH
SIDE = 4
GROUPS = SIDE * SIDE
LINE = 2 * SIDE
SNAPS = 16
CYCLES = 256
ANGLES = 1024
ORDERS = 128
HALF = ORDERS // 2
CHUNK = 4


def make_table():
    order_index = np.arange(ORDERS)
    angle_index = np.arange(ANGLES)
    phase_index = order_index[:, None] * angle_index[None, :] % ANGLES
    radians = phase_index.astype(np.float32) * np.float32(2.0 * math.pi / ANGLES)
    norming = np.float32(math.sqrt(2.0 / ANGLES))
    table = np.concatenate([np.cos(radians) * norming, -np.sin(radians) * norming], axis=0)
    return table.astype(jnp.bfloat16)


HOPS = sorted(
    [(hx, hy, hz) for hx in (2, 1, 0) for hy in (2, 1, 0) for hz in (2, 1, 0)],
    key=lambda hops: (-hops[1] - hops[2], -hops[0]),
)


def for_each_offset(visit):
    for hops in HOPS:

        def step(k, carry, hops=hops):
            signs = k // 2
            offsets = []
            for h in hops:
                if h == 1:
                    offsets.append(1 + 2 * (signs % 2))
                    signs = signs // 2
                else:
                    offsets.append(h)
            visit(offsets[0], k % 2, offsets[1], offsets[2])
            return carry

        lax.fori_loop(0 if sum(hops) else 1, 2 * 2 ** sum(h == 1 for h in hops), step, 0)


CHIPS = sorted(
    [(dx, dy, dz) for dx in range(SIDE) for dy in range(SIDE) for dz in range(SIDE) if dx + dy + dz],
    key=lambda offset: -sum(min(d, SIDE - d) for d in offset),
)

SLOTS = sorted(
    [(dy, dz) for dy in range(SIDE) for dz in range(SIDE)],
    key=lambda offset: [-sum(min(d, SIDE - d) for d in offset)] + [-min(d, SIDE - d) for d in offset],
)


def kernel(
    img_hbm, msk_hbm, wts_hbm, inv_hbm, tab_hbm, out_ref,
    img, tab, msk, wts, inv, spectra, coeffs, arrived, counts, all_counts, all_wts, gram, tiles, kams,
    in_sems, img_sems, w_send, w_recv, a_send, a_recv, n_send, n_recv, g_send, g_recv, h_send, h_recv, k_send, k_recv,
):
    s = lax.axis_index("snap")
    o = lax.axis_index("ord")
    y, z = s // SIDE, s % SIDE
    x, c = o // 2, o % 2
    x_row, x_lane = x // 2, x % 2

    small = [
        pltpu.make_async_copy(src, dst, in_sems.at[k])
        for k, (src, dst) in enumerate(
            [(tab_hbm, tab), (msk_hbm, msk), (wts_hbm, wts), (inv_hbm, inv)]
        )
    ]
    small[0].start()
    for k in range(SNAPS // CHUNK):
        part = pl.ds(k * CHUNK, CHUNK)
        pltpu.make_async_copy(img_hbm.at[part], img.at[part], img_sems.at[k]).start()
        if k == 0:
            for copy in small[1:]:
                copy.start()

    x_at = [(x + d) % SIDE for d in range(SIDE)]
    y_at = [(y + d) % SIDE * SIDE for d in range(SIDE)]
    z_at = [(z + d) % SIDE for d in range(SIDE)]
    barrier = pltpu.get_barrier_semaphore()
    for dx, dy, dz in CHIPS + [(0, 0, 0)]:
        for dc in (0, 1):
            if dx or dy or dz or dc:
                there = (y_at[dy] + z_at[dz], x_at[dx] * 2 + (c if dc == 0 else 1 - c))
                pl.semaphore_signal(barrier, inc=1, device_id=there, device_id_type=MESH)

    for copy in small[:3]:
        copy.wait()

    def transform(chunk, carry):
        first = chunk * CHUNK
        loads = img.at[pl.ds(first, CHUNK)]
        pltpu.make_async_copy(loads, loads, img_sems.at[chunk]).wait()
        for u in range(CHUNK):
            k = first + u
            product = lax.dot_general(
                tab[...], img[k], (((1,), (1,)), ((), ())), preferred_element_type=jnp.float32
            )
            product = product * msk[pl.ds(o * SNAPS + k, 1), :].astype(jnp.float32)
            place = pl.multiple_of(k * 2 * ORDERS, 2 * ORDERS)
            for lane in range(2):
                spectra[lane, pl.ds(place, 2 * ORDERS), :] = product[:, 128 * lane : 128 * lane + 128]
        return carry

    lax.fori_loop(0, SNAPS // CHUNK, transform, 0)

    pl.semaphore_wait(barrier, GROUPS * LINE - 1)

    for dx, dy, dz in CHIPS:
        if dx == 0:
            pltpu.make_async_remote_copy(
                wts, all_wts.at[SIDE * dy + dz], w_send, w_recv,
                device_id=(y_at[dy] + z_at[dz], o), device_id_type=MESH,
            ).start()
    all_wts[0] = wts[...]

    def gather(order):
        for part in range(2):
            for lane in range(2):
                rows = spectra[lane, pl.ds(part * ORDERS + order, SNAPS, stride=2 * ORDERS), :]
                coeffs[order, part, :, 128 * lane : 128 * lane + 128] = rows.astype(jnp.bfloat16)

    own_order = c * HALF + x * GROUPS + s
    gather(own_order)
    pltpu.make_async_copy(coeffs.at[own_order], arrived.at[0, :, o], a_recv.at[0]).start()

    def send_coeffs(dx, dc, dy, dz):
        group = (y + dy) % SIDE * SIDE + (z + dz) % SIDE
        there_x, there_c = (x + dx) % SIDE, (c + dc) % 2
        order = there_c * HALF + there_x * GROUPS + group
        gather(order)
        slot = SIDE * dy + dz
        pltpu.make_async_remote_copy(
            coeffs.at[order], arrived.at[slot, :, o], a_send, a_recv.at[slot],
            device_id=(group, there_x * 2 + there_c), device_id_type=MESH,
        ).start()

    for_each_offset(send_coeffs)

    small[3].wait()
    mask = msk[...].astype(jnp.float32)
    mask_half = msk[:, pl.ds(pl.multiple_of(x_lane * 128, 128), 128)].astype(jnp.float32)
    counts[...] = jnp.dot(
        mask.T * wts[...], mask_half,
        precision=lax.Precision.HIGHEST, preferred_element_type=jnp.float32,
    )

    def count_tile(group):
        return counts.at[pl.ds(pl.multiple_of(16 * group + 8 * x_row, 8), 8), :]

    pltpu.make_async_copy(all_wts.at[pl.ds(1, 15)], all_wts.at[pl.ds(1, 15)], w_recv).wait()
    gram[...] = jnp.zeros_like(gram)

    for dy, dz in SLOTS:
        slot = SIDE * dy + dz
        pltpu.make_async_copy(arrived.at[slot], arrived.at[slot], a_recv.at[slot]).wait()
        block = arrived[slot].reshape(2 * LINE * SNAPS, CYCLES)
        weight = jnp.concatenate([all_wts[slot], all_wts[slot]], axis=1)
        weighted = (block.astype(jnp.float32).T * weight).astype(jnp.bfloat16)
        gram[...] += jnp.dot(weighted, block, preferred_element_type=jnp.float32)

    tile_rows = pl.ds(pl.multiple_of(8 * own_order, 8), 8)

    def gram_tile(group, chip):
        row = pl.multiple_of(16 * group + 8 * (chip // 2), 8)
        lane = pl.multiple_of(128 * (chip % 2), 128)
        return gram.at[pl.ds(row, 8), pl.ds(lane, 128)]

    for dx, dy, dz in CHIPS:
        there_x = x_at[dx]
        group = y_at[dy] + z_at[dz]
        pltpu.make_async_remote_copy(
            gram_tile(group, there_x), tiles.at[tile_rows], g_send, g_recv.at[dx],
            device_id=(group, there_x * 2 + c), device_id_type=MESH,
        ).start()
    pltpu.make_async_copy(gram_tile(s, x), tiles.at[tile_rows], g_recv.at[0]).start()

    for dx, dy, dz in CHIPS:
        if dx == 0:
            group = y_at[dy] + z_at[dz]
            pltpu.make_async_remote_copy(
                count_tile(group), all_counts.at[SIDE * dy + dz], n_send, n_recv,
                device_id=(group, o), device_id_type=MESH,
            ).start()
    pltpu.make_async_copy(count_tile(s), all_counts.at[0], n_recv).start()

    for wave in range(SIDE):
        dx = (2, 1, 3, 0)[wave]
        row = pl.multiple_of(8 * (c * HALF + ((x + SIDE - dx) % SIDE) * GROUPS), 8 * GROUPS)
        part = tiles.at[pl.ds(row, 8 * GROUPS)]
        pltpu.make_async_copy(part, part, g_recv.at[dx]).wait()
        swap = pltpu.make_async_remote_copy(
            part, part, h_send, h_recv, device_id=(s, x * 2 + 1 - c), device_id_type=MESH
        )
        swap.start()
    own_inv = jnp.concatenate(
        [inv[pl.ds(pl.multiple_of(32 * k + 16 * c, 16), 16), :] for k in range(SIDE)], axis=0
    )
    own_half = tiles.at[pl.ds(pl.multiple_of(8 * HALF * c, 8 * HALF), 8 * HALF)]
    other_half = tiles.at[pl.ds(pl.multiple_of(8 * HALF * (1 - c), 8 * HALF), 8 * HALF)]
    pltpu.make_async_copy(own_half, own_half, h_send).wait()
    pltpu.make_async_copy(other_half, other_half, h_recv).wait()

    pltpu.make_async_copy(all_counts, all_counts, n_recv).wait()
    count = jnp.maximum(jnp.sum(all_counts[...], axis=0), 1.0)

    flat_kams = kams.reshape(HALF * 8, 128)
    for r in range(8):
        grams = tiles[pl.ds(r, ORDERS, stride=8), :]
        correl = grams / count[r : r + 1, :]
        flat_kams[pl.ds(r, HALF, stride=8), :] = jnp.dot(
            own_inv, correl, precision=lax.Precision.HIGHEST, preferred_element_type=jnp.float32
        )

    place = out_ref.at[:, pl.ds(pl.multiple_of(8 * x_row, 8), 8), pl.ds(pl.multiple_of(128 * x_lane, 128), 128)]
    for d in (2, 1, 3):
        there_x = (x + d) % SIDE
        pltpu.make_async_remote_copy(
            kams.at[pl.ds(16 * there_x, 16)], place, k_send, k_recv,
            device_id=(s, there_x * 2 + c), device_id_type=MESH,
        ).start()
    pltpu.make_async_copy(kams.at[pl.ds(16 * x, 16)], place, k_recv).start()

    pltpu.make_async_copy(all_wts.at[pl.ds(0, 15)], all_wts.at[pl.ds(0, 15)], w_send).wait()
    pltpu.make_async_copy(all_counts.at[pl.ds(0, 15)], all_counts.at[pl.ds(0, 15)], n_send).wait()
    pltpu.make_async_copy(coeffs.at[pl.ds(0, 127)], coeffs.at[pl.ds(0, 127)], a_send).wait()
    pltpu.make_async_copy(tiles.at[pl.ds(0, 504)], tiles.at[pl.ds(0, 504)], g_send).wait()
    pltpu.make_async_copy(kams.at[pl.ds(0, 48)], kams.at[pl.ds(0, 48)], k_send).wait()
    pltpu.make_async_copy(out_ref, out_ref, k_recv).wait()


def on_device(images, cycle_masks, weights, inversion):
    operands = (images, cycle_masks, weights.reshape(1, -1), inversion, jnp.asarray(make_table()))
    dma = pltpu.SemaphoreType.DMA
    f32, bf16 = jnp.float32, jnp.bfloat16
    return pl.pallas_call(
        kernel,
        out_shape=pltpu.VMEM((16, 16, CYCLES), f32),
        in_specs=[pl.BlockSpec(memory_space=pltpu.HBM)] * 5,
        out_specs=pl.BlockSpec(memory_space=pltpu.VMEM),
        scratch_shapes=[
            pltpu.VMEM((SNAPS, CYCLES, ANGLES), bf16),
            pltpu.VMEM((2 * ORDERS, ANGLES), bf16),
            pltpu.VMEM((LINE * SNAPS, CYCLES), jnp.int32),
            pltpu.VMEM((1, LINE * SNAPS), f32),
            pltpu.VMEM((ORDERS, ORDERS), f32),
            pltpu.VMEM((2, SNAPS * 2 * ORDERS, 128), f32),
            pltpu.VMEM((ORDERS, 2, SNAPS, CYCLES), bf16),
            pltpu.VMEM((GROUPS, 2, LINE, SNAPS, CYCLES), bf16),
            pltpu.VMEM((CYCLES, 128), f32),
            pltpu.VMEM((GROUPS, 8, 128), f32),
            pltpu.VMEM((GROUPS, 1, LINE * SNAPS), f32),
            pltpu.VMEM((CYCLES, CYCLES), f32),
            pltpu.VMEM((ORDERS * 8, 128), f32),
            pltpu.VMEM((HALF, 8, 128), f32),
            dma((4,)),
            dma((SNAPS // CHUNK,)),
            dma, dma, dma,
            dma((GROUPS,)),
            dma, dma, dma,
            dma((SIDE,)),
            dma, dma, dma, dma,
        ],
        compiler_params=pltpu.CompilerParams(
            collective_id=0, has_side_effects=True, vmem_limit_bytes=48 * 2**20
        ),
        name="kam",
    )(*(pltpu.with_memory_space_constraint(value, pltpu.HBM) for value in operands))


def solution(mesh):
    placed = (P(("snap", "ord"), None, None), P("snap", None), P("snap"), P())
    return jax.shard_map(
        on_device, mesh=mesh, in_specs=placed, out_specs=P("ord", "snap", None), check_vma=False
    )
```

```python
import functools
import math

import jax
import jax.numpy as jnp
import numpy as np
from jax import lax
from jax.experimental import pallas as pl
from jax.experimental.pallas import tpu as pltpu
from jax.sharding import PartitionSpec as P

MESH = pl.DeviceIdType.MESH
SIDE = 4
GROUPS = SIDE * SIDE
LINE = 2 * SIDE
SNAPS = 16
CYCLES = 256
ANGLES = 1024
ORDERS = 128
HALF = ORDERS // 2
CHUNK = 4


def make_table():
    order_index = np.arange(ORDERS)
    angle_index = np.arange(ANGLES)
    phase_index = order_index[:, None] * angle_index[None, :] % ANGLES
    radians = phase_index.astype(np.float32) * np.float32(2.0 * math.pi / ANGLES)
    norming = np.float32(math.sqrt(2.0 / ANGLES))
    table = np.concatenate([np.cos(radians) * norming, -np.sin(radians) * norming], axis=0)
    return table.astype(jnp.bfloat16)


HOPS = sorted(
    [(hx, hy, hz) for hx in (2, 1, 0) for hy in (2, 1, 0) for hz in (2, 1, 0)],
    key=lambda hops: (-hops[1] - hops[2], -hops[0]),
)


def for_each_offset(visit):
    for hops in HOPS:

        def step(k, carry, hops=hops):
            signs = k // 2
            offsets = []
            for h in hops:
                if h == 1:
                    offsets.append(1 + 2 * (signs % 2))
                    signs = signs // 2
                else:
                    offsets.append(h)
            sign_y, sign_z = [d // 3 if h == 1 else 0 for d, h in zip(offsets[1:], hops[1:])]
            slot = SLOT_BASE[hops[1:]] + sign_y + (2 if hops[1] == 1 else 1) * sign_z
            visit(offsets[0], k % 2, offsets[1], offsets[2], slot)
            return carry

        lax.fori_loop(0 if sum(hops) else 1, 2 * 2 ** sum(h == 1 for h in hops), step, 0)


CHIPS = sorted(
    [(dx, dy, dz) for dx in range(SIDE) for dy in range(SIDE) for dz in range(SIDE) if dx + dy + dz],
    key=lambda offset: -sum(min(d, SIDE - d) for d in offset),
)

SLOT_BASE = {}
for _, hop_y, hop_z in HOPS:
    if (hop_y, hop_z) not in SLOT_BASE:
        SLOT_BASE[hop_y, hop_z] = sum(2 ** ((u == 1) + (v == 1)) for u, v in SLOT_BASE)
RUNS = ((0, 1), (1, 4), (5, 6), (11, 5))


OWN_SLOT = GROUPS - 1


def slot_of(dy, dz):
    hop_y, hop_z = min(dy, SIDE - dy), min(dz, SIDE - dz)
    sign_y, sign_z = dy // 3, dz // 3
    return SLOT_BASE[hop_y, hop_z] + sign_y + (2 if hop_y == 1 else 1) * sign_z


def kernel(
    img_hbm, msk_hbm, wts_hbm, inv_hbm, tab_hbm, out_ref,
    img, tab, msk, wts, inv, spectra, coeffs, arrived, counts, all_counts, all_wts, gram, tiles, kams,
    in_sems, img_sems, w_send, w_recv, a_send, a_recv, n_send, n_recv, g_send, g_recv, h_send, h_recv, k_send, k_recv,
):
    s = lax.axis_index("snap")
    o = lax.axis_index("ord")
    y, z = s // SIDE, s % SIDE
    x, c = o // 2, o % 2
    x_row, x_lane = x // 2, x % 2

    small = [
        pltpu.make_async_copy(src, dst, in_sems.at[k])
        for k, (src, dst) in enumerate(
            [(tab_hbm, tab), (msk_hbm, msk), (wts_hbm, wts), (inv_hbm, inv)]
        )
    ]
    small[0].start()
    for k in range(SNAPS // CHUNK):
        part = pl.ds(k * CHUNK, CHUNK)
        pltpu.make_async_copy(img_hbm.at[part], img.at[part], img_sems.at[k]).start()
        if k == 0:
            for copy in small[1:]:
                copy.start()

    x_at = [(x + d) % SIDE for d in range(SIDE)]
    y_at = [(y + d) % SIDE * SIDE for d in range(SIDE)]
    z_at = [(z + d) % SIDE for d in range(SIDE)]
    barrier = pltpu.get_barrier_semaphore()
    for dx, dy, dz in CHIPS + [(0, 0, 0)]:
        for dc in (0, 1):
            if dx or dy or dz or dc:
                there = (y_at[dy] + z_at[dz], x_at[dx] * 2 + (c if dc == 0 else 1 - c))
                pl.semaphore_signal(barrier, inc=1, device_id=there, device_id_type=MESH)

    for copy in small[:3]:
        copy.wait()

    def transform(chunk, carry):
        first = chunk * CHUNK
        loads = img.at[pl.ds(first, CHUNK)]
        pltpu.make_async_copy(loads, loads, img_sems.at[chunk]).wait()
        for u in range(CHUNK):
            k = first + u
            product = lax.dot_general(
                tab[...], img[k], (((1,), (1,)), ((), ())), preferred_element_type=jnp.float32
            )
            product = product * msk[pl.ds(o * SNAPS + k, 1), :].astype(jnp.float32)
            place = pl.multiple_of(k * 2 * ORDERS, 2 * ORDERS)
            for lane in range(2):
                spectra[lane, pl.ds(place, 2 * ORDERS), :] = product[:, 128 * lane : 128 * lane + 128]
        return carry

    lax.fori_loop(0, SNAPS // CHUNK, transform, 0)

    pl.semaphore_wait(barrier, GROUPS * LINE - 1)

    for dx, dy, dz in CHIPS:
        if dx == 0:
            pltpu.make_async_remote_copy(
                wts, all_wts.at[slot_of(dy, dz)], w_send, w_recv,
                device_id=(y_at[dy] + z_at[dz], o), device_id_type=MESH,
            ).start()
    all_wts[OWN_SLOT] = wts[...]

    def gather(order):
        for part in range(2):
            for lane in range(2):
                rows = spectra[lane, pl.ds(part * ORDERS + order, SNAPS, stride=2 * ORDERS), :]
                coeffs[order, part, :, 128 * lane : 128 * lane + 128] = rows.astype(jnp.bfloat16)

    own_order = c * HALF + x * GROUPS + s
    gather(own_order)
    pltpu.make_async_copy(coeffs.at[own_order], arrived.at[OWN_SLOT, :, o], a_recv.at[OWN_SLOT]).start()

    def send_coeffs(dx, dc, dy, dz, slot):
        group = (y + dy) % SIDE * SIDE + (z + dz) % SIDE
        there_x, there_c = (x + dx) % SIDE, (c + dc) % 2
        order = there_c * HALF + there_x * GROUPS + group
        gather(order)
        pltpu.make_async_remote_copy(
            coeffs.at[order], arrived.at[slot, :, o], a_send, a_recv.at[slot],
            device_id=(group, there_x * 2 + there_c), device_id_type=MESH,
        ).start()

    for_each_offset(send_coeffs)

    small[3].wait()
    mask = msk[...].astype(jnp.float32)
    mask_half = msk[:, pl.ds(pl.multiple_of(x_lane * 128, 128), 128)].astype(jnp.float32)
    counts[...] = jnp.dot(
        mask.T * wts[...], mask_half,
        precision=lax.Precision.HIGHEST, preferred_element_type=jnp.float32,
    )

    def count_tile(group):
        return counts.at[pl.ds(pl.multiple_of(16 * group + 8 * x_row, 8), 8), :]

    pltpu.make_async_copy(all_wts.at[pl.ds(0, 15)], all_wts.at[pl.ds(0, 15)], w_recv).wait()

    for first, count in RUNS:
        for slot in range(first, first + count):
            pltpu.make_async_copy(arrived.at[slot], arrived.at[slot], a_recv.at[slot]).wait()
        block = arrived[first : first + count].reshape(count * 2 * LINE * SNAPS, CYCLES)
        weight = jnp.concatenate([all_wts[first + k // 2] for k in range(2 * count)], axis=1)
        weighted = (block.T.astype(jnp.float32) * weight).astype(jnp.bfloat16)
        product = jnp.dot(weighted, block, preferred_element_type=jnp.float32)
        gram[...] = product if first == 0 else gram[...] + product

    tile_rows = pl.ds(pl.multiple_of(8 * own_order, 8), 8)

    def gram_tile(group, chip):
        row = pl.multiple_of(16 * group + 8 * (chip // 2), 8)
        lane = pl.multiple_of(128 * (chip % 2), 128)
        return gram.at[pl.ds(row, 8), pl.ds(lane, 128)]

    for dx, dy, dz in CHIPS:
        there_x = x_at[dx]
        group = y_at[dy] + z_at[dz]
        pltpu.make_async_remote_copy(
            gram_tile(group, there_x), tiles.at[tile_rows], g_send, g_recv.at[dx],
            device_id=(group, there_x * 2 + c), device_id_type=MESH,
        ).start()
    pltpu.make_async_copy(gram_tile(s, x), tiles.at[tile_rows], g_recv.at[0]).start()

    for dx, dy, dz in CHIPS:
        if dx == 0:
            group = y_at[dy] + z_at[dz]
            pltpu.make_async_remote_copy(
                count_tile(group), all_counts.at[slot_of(dy, dz)], n_send, n_recv,
                device_id=(group, o), device_id_type=MESH,
            ).start()
    pltpu.make_async_copy(count_tile(s), all_counts.at[OWN_SLOT], n_recv).start()

    for wave in range(SIDE):
        dx = (2, 1, 3, 0)[wave]
        row = pl.multiple_of(8 * (c * HALF + ((x + SIDE - dx) % SIDE) * GROUPS), 8 * GROUPS)
        part = tiles.at[pl.ds(row, 8 * GROUPS)]
        pltpu.make_async_copy(part, part, g_recv.at[dx]).wait()
        swap = pltpu.make_async_remote_copy(
            part, part, h_send, h_recv, device_id=(s, x * 2 + 1 - c), device_id_type=MESH
        )
        swap.start()
    own_inv = jnp.concatenate(
        [inv[pl.ds(pl.multiple_of(32 * k + 16 * c, 16), 16), :] for k in range(SIDE)], axis=0
    )
    own_half = tiles.at[pl.ds(pl.multiple_of(8 * HALF * c, 8 * HALF), 8 * HALF)]
    other_half = tiles.at[pl.ds(pl.multiple_of(8 * HALF * (1 - c), 8 * HALF), 8 * HALF)]
    pltpu.make_async_copy(own_half, own_half, h_send).wait()
    pltpu.make_async_copy(other_half, other_half, h_recv).wait()

    pltpu.make_async_copy(all_counts, all_counts, n_recv).wait()
    count = jnp.maximum(jnp.sum(all_counts[...], axis=0), 1.0)

    flat_kams = kams.reshape(HALF * 8, 128)
    for r in range(8):
        grams = tiles[pl.ds(r, ORDERS, stride=8), :]
        correl = grams / count[r : r + 1, :]
        flat_kams[pl.ds(r, HALF, stride=8), :] = jnp.dot(
            own_inv, correl, precision=lax.Precision.HIGHEST, preferred_element_type=jnp.float32
        )

    place = out_ref.at[:, pl.ds(pl.multiple_of(8 * x_row, 8), 8), pl.ds(pl.multiple_of(128 * x_lane, 128), 128)]
    for d in (2, 1, 3):
        there_x = (x + d) % SIDE
        pltpu.make_async_remote_copy(
            kams.at[pl.ds(16 * there_x, 16)], place, k_send, k_recv,
            device_id=(s, there_x * 2 + c), device_id_type=MESH,
        ).start()
    pltpu.make_async_copy(kams.at[pl.ds(16 * x, 16)], place, k_recv).start()

    pltpu.make_async_copy(all_wts.at[pl.ds(0, 15)], all_wts.at[pl.ds(0, 15)], w_send).wait()
    pltpu.make_async_copy(all_counts.at[pl.ds(0, 15)], all_counts.at[pl.ds(0, 15)], n_send).wait()
    pltpu.make_async_copy(coeffs.at[pl.ds(0, 127)], coeffs.at[pl.ds(0, 127)], a_send).wait()
    pltpu.make_async_copy(tiles.at[pl.ds(0, 504)], tiles.at[pl.ds(0, 504)], g_send).wait()
    pltpu.make_async_copy(kams.at[pl.ds(0, 48)], kams.at[pl.ds(0, 48)], k_send).wait()
    pltpu.make_async_copy(out_ref, out_ref, k_recv).wait()


def on_device(images, cycle_masks, weights, inversion):
    operands = (images, cycle_masks, weights.reshape(1, -1), inversion, jnp.asarray(make_table()))
    dma = pltpu.SemaphoreType.DMA
    f32, bf16 = jnp.float32, jnp.bfloat16
    return pl.pallas_call(
        kernel,
        out_shape=pltpu.VMEM((16, 16, CYCLES), f32),
        in_specs=[pl.BlockSpec(memory_space=pltpu.HBM)] * 5,
        out_specs=pl.BlockSpec(memory_space=pltpu.VMEM),
        scratch_shapes=[
            pltpu.VMEM((SNAPS, CYCLES, ANGLES), bf16),
            pltpu.VMEM((2 * ORDERS, ANGLES), bf16),
            pltpu.VMEM((LINE * SNAPS, CYCLES), jnp.int32),
            pltpu.VMEM((1, LINE * SNAPS), f32),
            pltpu.VMEM((ORDERS, ORDERS), f32),
            pltpu.VMEM((2, SNAPS * 2 * ORDERS, 128), f32),
            pltpu.VMEM((ORDERS, 2, SNAPS, CYCLES), bf16),
            pltpu.VMEM((GROUPS, 2, LINE, SNAPS, CYCLES), bf16),
            pltpu.VMEM((CYCLES, 128), f32),
            pltpu.VMEM((GROUPS, 8, 128), f32),
            pltpu.VMEM((GROUPS, 1, LINE * SNAPS), f32),
            pltpu.VMEM((CYCLES, CYCLES), f32),
            pltpu.VMEM((ORDERS * 8, 128), f32),
            pltpu.VMEM((HALF, 8, 128), f32),
            dma((4,)),
            dma((SNAPS // CHUNK,)),
            dma, dma, dma,
            dma((GROUPS,)),
            dma, dma, dma,
            dma((SIDE,)),
            dma, dma, dma, dma,
        ],
        compiler_params=pltpu.CompilerParams(
            collective_id=0, has_side_effects=True, vmem_limit_bytes=48 * 2**20
        ),
        name="kam",
    )(*(pltpu.with_memory_space_constraint(value, pltpu.HBM) for value in operands))


def solution(mesh):
    placed = (P(("snap", "ord"), None, None), P("snap", None), P("snap"), P())
    return jax.shard_map(
        on_device, mesh=mesh, in_specs=placed, out_specs=P("ord", "snap", None), check_vma=False
    )
```

```python
import functools
import math

import jax
import jax.numpy as jnp
import numpy as np
from jax import lax
from jax.experimental import pallas as pl
from jax.experimental.pallas import tpu as pltpu
from jax.sharding import PartitionSpec as P

MESH = pl.DeviceIdType.MESH
SIDE = 4
GROUPS = SIDE * SIDE
LINE = 2 * SIDE
SNAPS = 16
CYCLES = 256
ANGLES = 1024
ORDERS = 128
HALF = ORDERS // 2
CHUNK = 4


def make_table():
    order_index = np.arange(ORDERS)
    angle_index = np.arange(ANGLES)
    phase_index = order_index[:, None] * angle_index[None, :] % ANGLES
    radians = phase_index.astype(np.float32) * np.float32(2.0 * math.pi / ANGLES)
    norming = np.float32(math.sqrt(2.0 / ANGLES))
    table = np.concatenate([np.cos(radians) * norming, -np.sin(radians) * norming], axis=0)
    return table.astype(jnp.bfloat16)


HOPS = sorted(
    [(hx, hy, hz) for hx in (2, 1, 0) for hy in (2, 1, 0) for hz in (2, 1, 0)],
    key=lambda hops: (-hops[1] - hops[2], -hops[0]),
)


def for_each_offset(visit):
    for hops in HOPS:

        def step(k, carry, hops=hops):
            signs = k // 2
            offsets = []
            for h in hops:
                if h == 1:
                    offsets.append(1 + 2 * (signs % 2))
                    signs = signs // 2
                else:
                    offsets.append(h)
            sign_y, sign_z = [d // 3 if h == 1 else 0 for d, h in zip(offsets[1:], hops[1:])]
            slot = SLOT_BASE[hops[1:]] + sign_y + (2 if hops[1] == 1 else 1) * sign_z
            visit(offsets[0], k % 2, offsets[1], offsets[2], slot)
            return carry

        lax.fori_loop(0 if sum(hops) else 1, 2 * 2 ** sum(h == 1 for h in hops), step, 0)


CHIPS = sorted(
    [(dx, dy, dz) for dx in range(SIDE) for dy in range(SIDE) for dz in range(SIDE) if dx + dy + dz],
    key=lambda offset: -sum(min(d, SIDE - d) for d in offset),
)

SLOT_BASE = {}
for _, hop_y, hop_z in HOPS:
    if (hop_y, hop_z) not in SLOT_BASE:
        SLOT_BASE[hop_y, hop_z] = sum(2 ** ((u == 1) + (v == 1)) for u, v in SLOT_BASE)
RUNS = ((0, 1), (1, 4), (5, 6), (11, 5))


OWN_SLOT = GROUPS - 1


def slot_of(dy, dz):
    hop_y, hop_z = min(dy, SIDE - dy), min(dz, SIDE - dz)
    sign_y, sign_z = dy // 3, dz // 3
    return SLOT_BASE[hop_y, hop_z] + sign_y + (2 if hop_y == 1 else 1) * sign_z


def kernel(
    img_hbm, msk_hbm, wts_hbm, inv_hbm, tab_hbm, out_ref,
    img, tab, msk, wts, inv, spectra, coeffs, arrived, counts, all_counts, all_wts, gram, tiles, kams,
    in_sems, img_sems, w_send, w_recv, a_send, a_recv, n_send, n_recv, g_send, g_recv, h_send, h_recv, k_send, k_recv,
):
    s = lax.axis_index("snap")
    o = lax.axis_index("ord")
    y, z = s // SIDE, s % SIDE
    x, c = o // 2, o % 2
    x_row, x_lane = x // 2, x % 2

    small = [
        pltpu.make_async_copy(src, dst, in_sems.at[k])
        for k, (src, dst) in enumerate(
            [(tab_hbm, tab), (msk_hbm, msk), (wts_hbm, wts), (inv_hbm, inv)]
        )
    ]
    small[0].start()
    for k in range(SNAPS // CHUNK):
        part = pl.ds(k * CHUNK, CHUNK)
        pltpu.make_async_copy(img_hbm.at[part], img.at[part], img_sems.at[k]).start()
        if k == 0:
            for copy in small[1:]:
                copy.start()

    x_at = [(x + d) % SIDE for d in range(SIDE)]
    y_at = [(y + d) % SIDE * SIDE for d in range(SIDE)]
    z_at = [(z + d) % SIDE for d in range(SIDE)]
    barrier = pltpu.get_barrier_semaphore()
    for dx, dy, dz in CHIPS + [(0, 0, 0)]:
        for dc in (0, 1):
            if dx or dy or dz or dc:
                there = (y_at[dy] + z_at[dz], x_at[dx] * 2 + (c if dc == 0 else 1 - c))
                pl.semaphore_signal(barrier, inc=1, device_id=there, device_id_type=MESH)

    for copy in small[:3]:
        copy.wait()

    def transform(chunk, carry):
        first = chunk * CHUNK
        loads = img.at[pl.ds(first, CHUNK)]
        pltpu.make_async_copy(loads, loads, img_sems.at[chunk]).wait()
        for u in range(CHUNK):
            k = first + u
            product = lax.dot_general(
                tab[...], img[k], (((1,), (1,)), ((), ())), preferred_element_type=jnp.float32
            )
            product = product * msk[pl.ds(o * SNAPS + k, 1), :].astype(jnp.float32)
            place = pl.multiple_of(k * 2 * ORDERS, 2 * ORDERS)
            for lane in range(2):
                spectra[lane, pl.ds(place, 2 * ORDERS), :] = product[:, 128 * lane : 128 * lane + 128]
        return carry

    lax.fori_loop(0, SNAPS // CHUNK, transform, 0)

    pl.semaphore_wait(barrier, GROUPS * LINE - 1)

    for dx, dy, dz in CHIPS:
        if dx == 0:
            pltpu.make_async_remote_copy(
                wts, all_wts.at[slot_of(dy, dz)], w_send, w_recv,
                device_id=(y_at[dy] + z_at[dz], o), device_id_type=MESH,
            ).start()
    all_wts[OWN_SLOT] = wts[...]

    def gather(order):
        for part in range(2):
            for lane in range(2):
                rows = spectra[lane, pl.ds(part * ORDERS + order, SNAPS, stride=2 * ORDERS), :]
                coeffs[order, part, :, 128 * lane : 128 * lane + 128] = rows.astype(jnp.bfloat16)

    own_order = c * HALF + x * GROUPS + s
    gather(own_order)
    pltpu.make_async_copy(coeffs.at[own_order], arrived.at[OWN_SLOT, :, o], a_recv.at[OWN_SLOT]).start()

    def send_coeffs(dx, dc, dy, dz, slot):
        group = (y + dy) % SIDE * SIDE + (z + dz) % SIDE
        there_x, there_c = (x + dx) % SIDE, (c + dc) % 2
        order = there_c * HALF + there_x * GROUPS + group
        gather(order)
        pltpu.make_async_remote_copy(
            coeffs.at[order], arrived.at[slot, :, o], a_send, a_recv.at[slot],
            device_id=(group, there_x * 2 + there_c), device_id_type=MESH,
        ).start()

    for_each_offset(send_coeffs)

    small[3].wait()
    mask = msk[...].astype(jnp.float32)
    mask_half = msk[:, pl.ds(pl.multiple_of(x_lane * 128, 128), 128)].astype(jnp.float32)
    counts[...] = jnp.dot(
        mask.T * wts[...], mask_half,
        precision=lax.Precision.HIGHEST, preferred_element_type=jnp.float32,
    )

    def count_tile(group):
        return counts.at[pl.ds(pl.multiple_of(16 * group + 8 * x_row, 8), 8), :]

    pltpu.make_async_copy(all_wts.at[pl.ds(0, 15)], all_wts.at[pl.ds(0, 15)], w_recv).wait()

    for first, count in RUNS:
        for slot in range(first, first + count):
            pltpu.make_async_copy(arrived.at[slot], arrived.at[slot], a_recv.at[slot]).wait()
        block = arrived[first : first + count].reshape(count * 2 * LINE * SNAPS, CYCLES)
        weight = jnp.concatenate([all_wts[first + k // 2] for k in range(2 * count)], axis=1)
        weighted = (block.T.astype(jnp.float32) * weight).astype(jnp.bfloat16)
        product = jnp.dot(weighted, block, preferred_element_type=jnp.float32)
        gram[...] = product if first == 0 else gram[...] + product

    tile_rows = pl.ds(pl.multiple_of(8 * own_order, 8), 8)

    def gram_tile(group, chip):
        row = pl.multiple_of(16 * group + 8 * (chip // 2), 8)
        lane = pl.multiple_of(128 * (chip % 2), 128)
        return gram.at[pl.ds(row, 8), pl.ds(lane, 128)]

    for dx, dy, dz in CHIPS:
        there_x = x_at[dx]
        group = y_at[dy] + z_at[dz]
        pltpu.make_async_remote_copy(
            gram_tile(group, there_x), tiles.at[tile_rows], g_send, g_recv.at[dx],
            device_id=(group, there_x * 2 + c), device_id_type=MESH,
        ).start()
    pltpu.make_async_copy(gram_tile(s, x), tiles.at[tile_rows], g_recv.at[0]).start()

    for dx, dy, dz in CHIPS:
        if dx == 0:
            group = y_at[dy] + z_at[dz]
            pltpu.make_async_remote_copy(
                count_tile(group), all_counts.at[slot_of(dy, dz)], n_send, n_recv,
                device_id=(group, o), device_id_type=MESH,
            ).start()
    pltpu.make_async_copy(count_tile(s), all_counts.at[OWN_SLOT], n_recv).start()

    for wave in range(SIDE):
        dx = (2, 1, 3, 0)[wave]
        row = pl.multiple_of(8 * (c * HALF + ((x + SIDE - dx) % SIDE) * GROUPS), 8 * GROUPS)
        part = tiles.at[pl.ds(row, 8 * GROUPS)]
        pltpu.make_async_copy(part, part, g_recv.at[dx]).wait()
        swap = pltpu.make_async_remote_copy(
            part, part, h_send, h_recv, device_id=(s, x * 2 + 1 - c), device_id_type=MESH
        )
        swap.start()
    own_inv = jnp.concatenate(
        [inv[pl.ds(pl.multiple_of(32 * k + 16 * c, 16), 16), :] for k in range(SIDE)], axis=0
    )
    own_half = tiles.at[pl.ds(pl.multiple_of(8 * HALF * c, 8 * HALF), 8 * HALF)]
    other_half = tiles.at[pl.ds(pl.multiple_of(8 * HALF * (1 - c), 8 * HALF), 8 * HALF)]
    pltpu.make_async_copy(other_half, other_half, h_recv).wait()

    pltpu.make_async_copy(all_counts, all_counts, n_recv).wait()
    count = jnp.maximum(jnp.sum(all_counts[...], axis=0), 1.0)

    correl = jnp.concatenate(
        [tiles[pl.ds(r, ORDERS, stride=8), :] / count[r : r + 1, :] for r in range(8)], axis=1
    )
    product = jnp.dot(own_inv, correl, precision=lax.Precision.HIGHEST, preferred_element_type=jnp.float32)
    flat_kams = kams.reshape(HALF * 8, 128)
    for r in range(8):
        flat_kams[pl.ds(r, HALF, stride=8), :] = product[:, 128 * r : 128 * r + 128]

    place = out_ref.at[:, pl.ds(pl.multiple_of(8 * x_row, 8), 8), pl.ds(pl.multiple_of(128 * x_lane, 128), 128)]
    for d in (2, 1, 3):
        there_x = (x + d) % SIDE
        pltpu.make_async_remote_copy(
            kams.at[pl.ds(16 * there_x, 16)], place, k_send, k_recv,
            device_id=(s, there_x * 2 + c), device_id_type=MESH,
        ).start()
    pltpu.make_async_copy(kams.at[pl.ds(16 * x, 16)], place, k_recv).start()

    pltpu.make_async_copy(all_wts.at[pl.ds(0, 15)], all_wts.at[pl.ds(0, 15)], w_send).wait()
    pltpu.make_async_copy(all_counts.at[pl.ds(0, 15)], all_counts.at[pl.ds(0, 15)], n_send).wait()
    pltpu.make_async_copy(coeffs.at[pl.ds(0, 127)], coeffs.at[pl.ds(0, 127)], a_send).wait()
    pltpu.make_async_copy(tiles.at[pl.ds(0, 504)], tiles.at[pl.ds(0, 504)], g_send).wait()
    pltpu.make_async_copy(own_half, own_half, h_send).wait()
    pltpu.make_async_copy(kams.at[pl.ds(0, 48)], kams.at[pl.ds(0, 48)], k_send).wait()
    pltpu.make_async_copy(out_ref, out_ref, k_recv).wait()


def on_device(images, cycle_masks, weights, inversion):
    operands = (images, cycle_masks, weights.reshape(1, -1), inversion, jnp.asarray(make_table()))
    dma = pltpu.SemaphoreType.DMA
    f32, bf16 = jnp.float32, jnp.bfloat16
    return pl.pallas_call(
        kernel,
        out_shape=pltpu.VMEM((16, 16, CYCLES), f32),
        in_specs=[pl.BlockSpec(memory_space=pltpu.HBM)] * 5,
        out_specs=pl.BlockSpec(memory_space=pltpu.VMEM),
        scratch_shapes=[
            pltpu.VMEM((SNAPS, CYCLES, ANGLES), bf16),
            pltpu.VMEM((2 * ORDERS, ANGLES), bf16),
            pltpu.VMEM((LINE * SNAPS, CYCLES), jnp.int32),
            pltpu.VMEM((1, LINE * SNAPS), f32),
            pltpu.VMEM((ORDERS, ORDERS), f32),
            pltpu.VMEM((2, SNAPS * 2 * ORDERS, 128), f32),
            pltpu.VMEM((ORDERS, 2, SNAPS, CYCLES), bf16),
            pltpu.VMEM((GROUPS, 2, LINE, SNAPS, CYCLES), bf16),
            pltpu.VMEM((CYCLES, 128), f32),
            pltpu.VMEM((GROUPS, 8, 128), f32),
            pltpu.VMEM((GROUPS, 1, LINE * SNAPS), f32),
            pltpu.VMEM((CYCLES, CYCLES), f32),
            pltpu.VMEM((ORDERS * 8, 128), f32),
            pltpu.VMEM((HALF, 8, 128), f32),
            dma((4,)),
            dma((SNAPS // CHUNK,)),
            dma, dma, dma,
            dma((GROUPS,)),
            dma, dma, dma,
            dma((SIDE,)),
            dma, dma, dma, dma,
        ],
        compiler_params=pltpu.CompilerParams(
            collective_id=0, has_side_effects=True, vmem_limit_bytes=48 * 2**20
        ),
        name="kam",
    )(*(pltpu.with_memory_space_constraint(value, pltpu.HBM) for value in operands))


def solution(mesh):
    placed = (P(("snap", "ord"), None, None), P("snap", None), P("snap"), P())
    return jax.shard_map(
        on_device, mesh=mesh, in_specs=placed, out_specs=P("ord", "snap", None), check_vma=False
    )
```

```python
import functools
import math

import jax
import jax.numpy as jnp
import numpy as np
from jax import lax
from jax.experimental import pallas as pl
from jax.experimental.pallas import tpu as pltpu
from jax.sharding import PartitionSpec as P

MESH = pl.DeviceIdType.MESH
SIDE = 4
GROUPS = SIDE * SIDE
LINE = 2 * SIDE
SNAPS = 16
CYCLES = 256
ANGLES = 1024
ORDERS = 128
HALF = ORDERS // 2
CHUNK = 4


def make_table():
    order_index = np.arange(ORDERS)
    angle_index = np.arange(ANGLES)
    phase_index = order_index[:, None] * angle_index[None, :] % ANGLES
    radians = phase_index.astype(np.float32) * np.float32(2.0 * math.pi / ANGLES)
    norming = np.float32(math.sqrt(2.0 / ANGLES))
    table = np.concatenate([np.cos(radians) * norming, -np.sin(radians) * norming], axis=0)
    return table.astype(jnp.bfloat16)


HOPS = sorted(
    [(hx, hy, hz) for hx in (2, 1, 0) for hy in (2, 1, 0) for hz in (2, 1, 0)],
    key=lambda hops: (-hops[1] - hops[2], -hops[0]),
)


FAR_HOPS, NEAR_HOPS = HOPS[:9], HOPS[9:]


def for_each_offset(visit, order):
    for hops in order:

        def step(k, carry, hops=hops):
            signs = k // 2
            offsets = []
            for h in hops:
                if h == 1:
                    offsets.append(1 + 2 * (signs % 2))
                    signs = signs // 2
                else:
                    offsets.append(h)
            sign_y, sign_z = [d // 3 if h == 1 else 0 for d, h in zip(offsets[1:], hops[1:])]
            slot = SLOT_BASE[hops[1:]] + sign_y + (2 if hops[1] == 1 else 1) * sign_z
            visit(offsets[0], k % 2, offsets[1], offsets[2], slot)
            return carry

        lax.fori_loop(0 if sum(hops) else 1, 2 * 2 ** sum(h == 1 for h in hops), step, 0)


CHIPS = sorted(
    [(dx, dy, dz) for dx in range(SIDE) for dy in range(SIDE) for dz in range(SIDE) if dx + dy + dz],
    key=lambda offset: -sum(min(d, SIDE - d) for d in offset),
)

SLOT_BASE = {}
for _, hop_y, hop_z in HOPS:
    if (hop_y, hop_z) not in SLOT_BASE:
        SLOT_BASE[hop_y, hop_z] = sum(2 ** ((u == 1) + (v == 1)) for u, v in SLOT_BASE)
RUNS = ((0, 1), (1, 4), (5, 6), (11, 5))


OWN_SLOT = GROUPS - 1


def slot_of(dy, dz):
    hop_y, hop_z = min(dy, SIDE - dy), min(dz, SIDE - dz)
    sign_y, sign_z = dy // 3, dz // 3
    return SLOT_BASE[hop_y, hop_z] + sign_y + (2 if hop_y == 1 else 1) * sign_z


def kernel(
    img_hbm, msk_hbm, wts_hbm, inv_hbm, tab_hbm, out_ref,
    img, tab, msk, wts, inv, spectra, coeffs, arrived, counts, all_counts, all_wts, gram, tiles, kams,
    in_sems, img_sems, w_send, w_recv, a_send, a_recv, n_send, n_recv, g_send, g_recv, h_send, h_recv, k_send, k_recv,
):
    s = lax.axis_index("snap")
    o = lax.axis_index("ord")
    y, z = s // SIDE, s % SIDE
    x, c = o // 2, o % 2
    x_row, x_lane = x // 2, x % 2

    small = [
        pltpu.make_async_copy(src, dst, in_sems.at[k])
        for k, (src, dst) in enumerate(
            [(tab_hbm, tab), (msk_hbm, msk), (wts_hbm, wts), (inv_hbm, inv)]
        )
    ]
    small[0].start()
    for k in range(SNAPS // CHUNK):
        part = pl.ds(k * CHUNK, CHUNK)
        pltpu.make_async_copy(img_hbm.at[part], img.at[part], img_sems.at[k]).start()
        if k == 0:
            for copy in small[1:]:
                copy.start()

    x_at = [(x + d) % SIDE for d in range(SIDE)]
    y_at = [(y + d) % SIDE * SIDE for d in range(SIDE)]
    z_at = [(z + d) % SIDE for d in range(SIDE)]
    barrier = pltpu.get_barrier_semaphore()
    for dx, dy, dz in CHIPS + [(0, 0, 0)]:
        for dc in (0, 1):
            if dx or dy or dz or dc:
                there = (y_at[dy] + z_at[dz], x_at[dx] * 2 + (c if dc == 0 else 1 - c))
                pl.semaphore_signal(barrier, inc=1, device_id=there, device_id_type=MESH)

    for copy in small[:3]:
        copy.wait()

    def transform(chunk, carry):
        first = chunk * CHUNK
        loads = img.at[pl.ds(first, CHUNK)]
        pltpu.make_async_copy(loads, loads, img_sems.at[chunk]).wait()
        for u in range(CHUNK):
            k = first + u
            product = lax.dot_general(
                tab[...], img[k], (((1,), (1,)), ((), ())), preferred_element_type=jnp.float32
            )
            product = product * msk[pl.ds(o * SNAPS + k, 1), :].astype(jnp.float32)
            place = pl.multiple_of(k * 2 * ORDERS, 2 * ORDERS)
            for lane in range(2):
                spectra[lane, pl.ds(place, 2 * ORDERS), :] = product[:, 128 * lane : 128 * lane + 128]
        return carry

    lax.fori_loop(0, SNAPS // CHUNK, transform, 0)

    pl.semaphore_wait(barrier, GROUPS * LINE - 1)

    all_wts[OWN_SLOT] = wts[...]

    def gather(order):
        for part in range(2):
            for lane in range(2):
                rows = spectra[lane, pl.ds(part * ORDERS + order, SNAPS, stride=2 * ORDERS), :]
                coeffs[order, part, :, 128 * lane : 128 * lane + 128] = rows.astype(jnp.bfloat16)

    own_order = c * HALF + x * GROUPS + s

    def send_coeffs(dx, dc, dy, dz, slot):
        group = (y + dy) % SIDE * SIDE + (z + dz) % SIDE
        there_x, there_c = (x + dx) % SIDE, (c + dc) % 2
        order = there_c * HALF + there_x * GROUPS + group
        gather(order)
        pltpu.make_async_remote_copy(
            coeffs.at[order], arrived.at[slot, :, o], a_send, a_recv.at[slot],
            device_id=(group, there_x * 2 + there_c), device_id_type=MESH,
        ).start()

    for_each_offset(send_coeffs, FAR_HOPS)
    for dx, dy, dz in CHIPS:
        if dx == 0:
            pltpu.make_async_remote_copy(
                wts, all_wts.at[slot_of(dy, dz)], w_send, w_recv,
                device_id=(y_at[dy] + z_at[dz], o), device_id_type=MESH,
            ).start()
    for_each_offset(send_coeffs, NEAR_HOPS)
    gather(own_order)
    pltpu.make_async_copy(coeffs.at[own_order], arrived.at[OWN_SLOT, :, o], a_recv.at[OWN_SLOT]).start()

    small[3].wait()
    mask = msk[...].astype(jnp.float32)
    mask_half = msk[:, pl.ds(pl.multiple_of(x_lane * 128, 128), 128)].astype(jnp.float32)
    counts[...] = jnp.dot(
        mask.T * wts[...], mask_half,
        precision=lax.Precision.HIGHEST, preferred_element_type=jnp.float32,
    )

    def count_tile(group):
        return counts.at[pl.ds(pl.multiple_of(16 * group + 8 * x_row, 8), 8), :]

    pltpu.make_async_copy(all_wts.at[pl.ds(0, 15)], all_wts.at[pl.ds(0, 15)], w_recv).wait()

    for first, count in RUNS:
        for slot in range(first, first + count):
            pltpu.make_async_copy(arrived.at[slot], arrived.at[slot], a_recv.at[slot]).wait()
        block = arrived[first : first + count].reshape(count * 2 * LINE * SNAPS, CYCLES)
        weight = jnp.concatenate([all_wts[first + k // 2] for k in range(2 * count)], axis=1)
        weighted = (block.T.astype(jnp.float32) * weight).astype(jnp.bfloat16)
        product = jnp.dot(weighted, block, preferred_element_type=jnp.float32)
        gram[...] = product if first == 0 else gram[...] + product

    tile_rows = pl.ds(pl.multiple_of(8 * own_order, 8), 8)

    def gram_tile(group, chip):
        row = pl.multiple_of(16 * group + 8 * (chip // 2), 8)
        lane = pl.multiple_of(128 * (chip % 2), 128)
        return gram.at[pl.ds(row, 8), pl.ds(lane, 128)]

    for dx, dy, dz in CHIPS:
        there_x = x_at[dx]
        group = y_at[dy] + z_at[dz]
        pltpu.make_async_remote_copy(
            gram_tile(group, there_x), tiles.at[tile_rows], g_send, g_recv.at[dx],
            device_id=(group, there_x * 2 + c), device_id_type=MESH,
        ).start()
    pltpu.make_async_copy(gram_tile(s, x), tiles.at[tile_rows], g_recv.at[0]).start()

    for dx, dy, dz in CHIPS:
        if dx == 0:
            group = y_at[dy] + z_at[dz]
            pltpu.make_async_remote_copy(
                count_tile(group), all_counts.at[slot_of(dy, dz)], n_send, n_recv,
                device_id=(group, o), device_id_type=MESH,
            ).start()
    pltpu.make_async_copy(count_tile(s), all_counts.at[OWN_SLOT], n_recv).start()

    for wave in range(SIDE):
        dx = (2, 1, 3, 0)[wave]
        row = pl.multiple_of(8 * (c * HALF + ((x + SIDE - dx) % SIDE) * GROUPS), 8 * GROUPS)
        part = tiles.at[pl.ds(row, 8 * GROUPS)]
        pltpu.make_async_copy(part, part, g_recv.at[dx]).wait()
        swap = pltpu.make_async_remote_copy(
            part, part, h_send, h_recv, device_id=(s, x * 2 + 1 - c), device_id_type=MESH
        )
        swap.start()
    own_inv = jnp.concatenate(
        [inv[pl.ds(pl.multiple_of(32 * k + 16 * c, 16), 16), :] for k in range(SIDE)], axis=0
    )
    own_half = tiles.at[pl.ds(pl.multiple_of(8 * HALF * c, 8 * HALF), 8 * HALF)]
    other_half = tiles.at[pl.ds(pl.multiple_of(8 * HALF * (1 - c), 8 * HALF), 8 * HALF)]
    pltpu.make_async_copy(all_counts, all_counts, n_recv).wait()
    count = jnp.maximum(jnp.sum(all_counts[...], axis=0), 1.0)
    pltpu.make_async_copy(other_half, other_half, h_recv).wait()


    correl = jnp.concatenate(
        [tiles[pl.ds(r, ORDERS, stride=8), :] / count[r : r + 1, :] for r in range(8)], axis=1
    )
    product = jnp.dot(own_inv, correl, precision=lax.Precision.HIGHEST, preferred_element_type=jnp.float32)
    flat_kams = kams.reshape(HALF * 8, 128)
    for r in range(8):
        flat_kams[pl.ds(r, HALF, stride=8), :] = product[:, 128 * r : 128 * r + 128]

    place = out_ref.at[:, pl.ds(pl.multiple_of(8 * x_row, 8), 8), pl.ds(pl.multiple_of(128 * x_lane, 128), 128)]
    for d in (2, 1, 3):
        there_x = (x + d) % SIDE
        pltpu.make_async_remote_copy(
            kams.at[pl.ds(16 * there_x, 16)], place, k_send, k_recv,
            device_id=(s, there_x * 2 + c), device_id_type=MESH,
        ).start()
    pltpu.make_async_copy(kams.at[pl.ds(16 * x, 16)], place, k_recv).start()

    pltpu.make_async_copy(all_wts.at[pl.ds(0, 15)], all_wts.at[pl.ds(0, 15)], w_send).wait()
    pltpu.make_async_copy(all_counts.at[pl.ds(0, 15)], all_counts.at[pl.ds(0, 15)], n_send).wait()
    pltpu.make_async_copy(coeffs.at[pl.ds(0, 127)], coeffs.at[pl.ds(0, 127)], a_send).wait()
    pltpu.make_async_copy(tiles.at[pl.ds(0, 504)], tiles.at[pl.ds(0, 504)], g_send).wait()
    pltpu.make_async_copy(own_half, own_half, h_send).wait()
    pltpu.make_async_copy(kams.at[pl.ds(0, 48)], kams.at[pl.ds(0, 48)], k_send).wait()
    pltpu.make_async_copy(out_ref, out_ref, k_recv).wait()


def on_device(images, cycle_masks, weights, inversion):
    operands = (images, cycle_masks, weights.reshape(1, -1), inversion, jnp.asarray(make_table()))
    dma = pltpu.SemaphoreType.DMA
    f32, bf16 = jnp.float32, jnp.bfloat16
    return pl.pallas_call(
        kernel,
        out_shape=pltpu.VMEM((16, 16, CYCLES), f32),
        in_specs=[pl.BlockSpec(memory_space=pltpu.HBM)] * 5,
        out_specs=pl.BlockSpec(memory_space=pltpu.VMEM),
        scratch_shapes=[
            pltpu.VMEM((SNAPS, CYCLES, ANGLES), bf16),
            pltpu.VMEM((2 * ORDERS, ANGLES), bf16),
            pltpu.VMEM((LINE * SNAPS, CYCLES), jnp.int32),
            pltpu.VMEM((1, LINE * SNAPS), f32),
            pltpu.VMEM((ORDERS, ORDERS), f32),
            pltpu.VMEM((2, SNAPS * 2 * ORDERS, 128), f32),
            pltpu.VMEM((ORDERS, 2, SNAPS, CYCLES), bf16),
            pltpu.VMEM((GROUPS, 2, LINE, SNAPS, CYCLES), bf16),
            pltpu.VMEM((CYCLES, 128), f32),
            pltpu.VMEM((GROUPS, 8, 128), f32),
            pltpu.VMEM((GROUPS, 1, LINE * SNAPS), f32),
            pltpu.VMEM((CYCLES, CYCLES), f32),
            pltpu.VMEM((ORDERS * 8, 128), f32),
            pltpu.VMEM((HALF, 8, 128), f32),
            dma((4,)),
            dma((SNAPS // CHUNK,)),
            dma, dma, dma,
            dma((GROUPS,)),
            dma, dma, dma,
            dma((SIDE,)),
            dma, dma, dma, dma,
        ],
        compiler_params=pltpu.CompilerParams(
            collective_id=0, has_side_effects=True, vmem_limit_bytes=48 * 2**20
        ),
        name="kam",
    )(*(pltpu.with_memory_space_constraint(value, pltpu.HBM) for value in operands))


def solution(mesh):
    placed = (P(("snap", "ord"), None, None), P("snap", None), P("snap"), P())
    return jax.shard_map(
        on_device, mesh=mesh, in_specs=placed, out_specs=P("ord", "snap", None), check_vma=False
    )
```

```python
import functools
import math

import jax
import jax.numpy as jnp
import numpy as np
from jax import lax
from jax.experimental import pallas as pl
from jax.experimental.pallas import tpu as pltpu
from jax.sharding import PartitionSpec as P

MESH = pl.DeviceIdType.MESH
SIDE = 4
GROUPS = SIDE * SIDE
LINE = 2 * SIDE
SNAPS = 16
CYCLES = 256
ANGLES = 1024
ORDERS = 128
HALF = ORDERS // 2
CHUNK = 4


def make_table():
    order_index = np.arange(ORDERS)
    angle_index = np.arange(ANGLES)
    phase_index = order_index[:, None] * angle_index[None, :] % ANGLES
    radians = phase_index.astype(np.float32) * np.float32(2.0 * math.pi / ANGLES)
    norming = np.float32(math.sqrt(2.0 / ANGLES))
    table = np.concatenate([np.cos(radians) * norming, -np.sin(radians) * norming], axis=0)
    return table.astype(jnp.bfloat16)


HOPS = sorted(
    [(hx, hy, hz) for hx in (2, 1, 0) for hy in (2, 1, 0) for hz in (2, 1, 0)],
    key=lambda hops: (-hops[1] - hops[2], -hops[0]),
)


FAR_HOPS, NEAR_HOPS = HOPS[:9], HOPS[9:]


def for_each_offset(visit, order):
    for hops in order:

        def step(k, carry, hops=hops):
            signs = k // 2
            offsets = []
            for h in hops:
                if h == 1:
                    offsets.append(1 + 2 * (signs % 2))
                    signs = signs // 2
                else:
                    offsets.append(h)
            sign_y, sign_z = [d // 3 if h == 1 else 0 for d, h in zip(offsets[1:], hops[1:])]
            slot = SLOT_BASE[hops[1:]] + sign_y + (2 if hops[1] == 1 else 1) * sign_z
            visit(offsets[0], k % 2, offsets[1], offsets[2], slot)
            return carry

        lax.fori_loop(0 if sum(hops) else 1, 2 * 2 ** sum(h == 1 for h in hops), step, 0)


CHIPS = sorted(
    [(dx, dy, dz) for dx in range(SIDE) for dy in range(SIDE) for dz in range(SIDE) if dx + dy + dz],
    key=lambda offset: -sum(min(d, SIDE - d) for d in offset),
)

SLOT_BASE = {}
for _, hop_y, hop_z in HOPS:
    if (hop_y, hop_z) not in SLOT_BASE:
        SLOT_BASE[hop_y, hop_z] = sum(2 ** ((u == 1) + (v == 1)) for u, v in SLOT_BASE)
RUNS = ((0, 1), (1, 4), (5, 6), (11, 5))


OWN_SLOT = GROUPS - 1


def slot_of(dy, dz):
    hop_y, hop_z = min(dy, SIDE - dy), min(dz, SIDE - dz)
    sign_y, sign_z = dy // 3, dz // 3
    return SLOT_BASE[hop_y, hop_z] + sign_y + (2 if hop_y == 1 else 1) * sign_z


def kernel(
    img_hbm, msk_hbm, wts_hbm, inv_hbm, tab_hbm, out_ref,
    img, tab, msk, wts, inv, spectra, coeffs, arrived, counts, all_counts, all_wts, gram, tiles, kams,
    in_sems, img_sems, w_send, w_recv, a_send, a_recv, n_send, n_recv, g_send, g_recv, h_send, h_recv, k_send, k_recv,
):
    s = lax.axis_index("snap")
    o = lax.axis_index("ord")
    y, z = s // SIDE, s % SIDE
    x, c = o // 2, o % 2
    x_row, x_lane = x // 2, x % 2

    small = [
        pltpu.make_async_copy(src, dst, in_sems.at[k])
        for k, (src, dst) in enumerate(
            [(tab_hbm, tab), (msk_hbm, msk), (wts_hbm, wts), (inv_hbm, inv)]
        )
    ]
    x_at = [(x + d) % SIDE for d in range(SIDE)]
    y_at = [(y + d) % SIDE * SIDE for d in range(SIDE)]
    z_at = [(z + d) % SIDE for d in range(SIDE)]
    barrier = pltpu.get_barrier_semaphore()

    def greet(chips):
        for dx, dy, dz in chips:
            for dc in (0, 1):
                if dx or dy or dz or dc:
                    there = (y_at[dy] + z_at[dz], x_at[dx] * 2 + (c if dc == 0 else 1 - c))
                    pl.semaphore_signal(barrier, inc=1, device_id=there, device_id_type=MESH)

    greet(CHIPS[:7])
    small[0].start()
    for k in range(SNAPS // CHUNK):
        part = pl.ds(k * CHUNK, CHUNK)
        pltpu.make_async_copy(img_hbm.at[part], img.at[part], img_sems.at[k]).start()
        if k == 0:
            for copy in small[1:]:
                copy.start()
    greet(CHIPS[7:] + [(0, 0, 0)])

    for copy in small[:3]:
        copy.wait()

    def transform(chunk, carry):
        first = chunk * CHUNK
        loads = img.at[pl.ds(first, CHUNK)]
        pltpu.make_async_copy(loads, loads, img_sems.at[chunk]).wait()
        for u in range(CHUNK):
            k = first + u
            product = lax.dot_general(
                tab[...], img[k], (((1,), (1,)), ((), ())), preferred_element_type=jnp.float32
            )
            product = product * msk[pl.ds(o * SNAPS + k, 1), :].astype(jnp.float32)
            place = pl.multiple_of(k * 2 * ORDERS, 2 * ORDERS)
            for lane in range(2):
                spectra[lane, pl.ds(place, 2 * ORDERS), :] = product[:, 128 * lane : 128 * lane + 128]
        return carry

    lax.fori_loop(0, SNAPS // CHUNK, transform, 0)

    pl.semaphore_wait(barrier, GROUPS * LINE - 1)

    all_wts[OWN_SLOT] = wts[...]

    def gather(order):
        for part in range(2):
            for lane in range(2):
                rows = spectra[lane, pl.ds(part * ORDERS + order, SNAPS, stride=2 * ORDERS), :]
                coeffs[order, part, :, 128 * lane : 128 * lane + 128] = rows.astype(jnp.bfloat16)

    own_order = c * HALF + x * GROUPS + s

    def send_coeffs(dx, dc, dy, dz, slot):
        group = (y + dy) % SIDE * SIDE + (z + dz) % SIDE
        there_x, there_c = (x + dx) % SIDE, (c + dc) % 2
        order = there_c * HALF + there_x * GROUPS + group
        gather(order)
        pltpu.make_async_remote_copy(
            coeffs.at[order], arrived.at[slot, :, o], a_send, a_recv.at[slot],
            device_id=(group, there_x * 2 + there_c), device_id_type=MESH,
        ).start()

    for_each_offset(send_coeffs, FAR_HOPS)
    for dx, dy, dz in CHIPS:
        if dx == 0:
            pltpu.make_async_remote_copy(
                wts, all_wts.at[slot_of(dy, dz)], w_send, w_recv,
                device_id=(y_at[dy] + z_at[dz], o), device_id_type=MESH,
            ).start()
    for_each_offset(send_coeffs, NEAR_HOPS)
    gather(own_order)
    pltpu.make_async_copy(coeffs.at[own_order], arrived.at[OWN_SLOT, :, o], a_recv.at[OWN_SLOT]).start()

    small[3].wait()
    mask = msk[...].astype(jnp.float32)
    mask_half = msk[:, pl.ds(pl.multiple_of(x_lane * 128, 128), 128)].astype(jnp.float32)
    counts[...] = jnp.dot(
        mask.T * wts[...], mask_half,
        precision=lax.Precision.HIGHEST, preferred_element_type=jnp.float32,
    )

    def count_tile(group):
        return counts.at[pl.ds(pl.multiple_of(16 * group + 8 * x_row, 8), 8), :]

    pltpu.make_async_copy(all_wts.at[pl.ds(0, 15)], all_wts.at[pl.ds(0, 15)], w_recv).wait()

    for first, count in RUNS:
        for slot in range(first, first + count):
            pltpu.make_async_copy(arrived.at[slot], arrived.at[slot], a_recv.at[slot]).wait()
        block = arrived[first : first + count].reshape(count * 2 * LINE * SNAPS, CYCLES)
        weight = jnp.concatenate([all_wts[first + k // 2] for k in range(2 * count)], axis=1)
        weighted = (block.T.astype(jnp.float32) * weight).astype(jnp.bfloat16)
        product = jnp.dot(weighted, block, preferred_element_type=jnp.float32)
        gram[...] = product if first == 0 else gram[...] + product

    tile_rows = pl.ds(pl.multiple_of(8 * own_order, 8), 8)

    def gram_tile(group, chip):
        row = pl.multiple_of(16 * group + 8 * (chip // 2), 8)
        lane = pl.multiple_of(128 * (chip % 2), 128)
        return gram.at[pl.ds(row, 8), pl.ds(lane, 128)]

    for dx, dy, dz in CHIPS:
        there_x = x_at[dx]
        group = y_at[dy] + z_at[dz]
        pltpu.make_async_remote_copy(
            gram_tile(group, there_x), tiles.at[tile_rows], g_send, g_recv.at[dx],
            device_id=(group, there_x * 2 + c), device_id_type=MESH,
        ).start()
    pltpu.make_async_copy(gram_tile(s, x), tiles.at[tile_rows], g_recv.at[0]).start()

    for dx, dy, dz in CHIPS:
        if dx == 0:
            group = y_at[dy] + z_at[dz]
            pltpu.make_async_remote_copy(
                count_tile(group), all_counts.at[slot_of(dy, dz)], n_send, n_recv,
                device_id=(group, o), device_id_type=MESH,
            ).start()
    pltpu.make_async_copy(count_tile(s), all_counts.at[OWN_SLOT], n_recv).start()

    for wave in range(SIDE):
        dx = (2, 1, 3, 0)[wave]
        row = pl.multiple_of(8 * (c * HALF + ((x + SIDE - dx) % SIDE) * GROUPS), 8 * GROUPS)
        part = tiles.at[pl.ds(row, 8 * GROUPS)]
        pltpu.make_async_copy(part, part, g_recv.at[dx]).wait()
        swap = pltpu.make_async_remote_copy(
            part, part, h_send, h_recv, device_id=(s, x * 2 + 1 - c), device_id_type=MESH
        )
        swap.start()
    own_inv = jnp.concatenate(
        [inv[pl.ds(pl.multiple_of(32 * k + 16 * c, 16), 16), :] for k in range(SIDE)], axis=0
    )
    own_half = tiles.at[pl.ds(pl.multiple_of(8 * HALF * c, 8 * HALF), 8 * HALF)]
    other_half = tiles.at[pl.ds(pl.multiple_of(8 * HALF * (1 - c), 8 * HALF), 8 * HALF)]
    pltpu.make_async_copy(all_counts, all_counts, n_recv).wait()
    count = jnp.maximum(jnp.sum(all_counts[...], axis=0), 1.0)
    pltpu.make_async_copy(other_half, other_half, h_recv).wait()


    correl = jnp.concatenate(
        [tiles[pl.ds(r, ORDERS, stride=8), :] / count[r : r + 1, :] for r in range(8)], axis=1
    )
    product = jnp.dot(own_inv, correl, precision=lax.Precision.HIGHEST, preferred_element_type=jnp.float32)
    flat_kams = kams.reshape(HALF * 8, 128)
    for r in range(8):
        flat_kams[pl.ds(r, HALF, stride=8), :] = product[:, 128 * r : 128 * r + 128]

    place = out_ref.at[:, pl.ds(pl.multiple_of(8 * x_row, 8), 8), pl.ds(pl.multiple_of(128 * x_lane, 128), 128)]
    for d in (2, 1, 3):
        there_x = (x + d) % SIDE
        pltpu.make_async_remote_copy(
            kams.at[pl.ds(16 * there_x, 16)], place, k_send, k_recv,
            device_id=(s, there_x * 2 + c), device_id_type=MESH,
        ).start()
    pltpu.make_async_copy(kams.at[pl.ds(16 * x, 16)], place, k_recv).start()

    pltpu.make_async_copy(all_wts.at[pl.ds(0, 15)], all_wts.at[pl.ds(0, 15)], w_send).wait()
    pltpu.make_async_copy(all_counts.at[pl.ds(0, 15)], all_counts.at[pl.ds(0, 15)], n_send).wait()
    pltpu.make_async_copy(coeffs.at[pl.ds(0, 127)], coeffs.at[pl.ds(0, 127)], a_send).wait()
    pltpu.make_async_copy(tiles.at[pl.ds(0, 504)], tiles.at[pl.ds(0, 504)], g_send).wait()
    pltpu.make_async_copy(own_half, own_half, h_send).wait()
    pltpu.make_async_copy(kams.at[pl.ds(0, 48)], kams.at[pl.ds(0, 48)], k_send).wait()
    pltpu.make_async_copy(out_ref, out_ref, k_recv).wait()


def on_device(images, cycle_masks, weights, inversion):
    operands = (images, cycle_masks, weights.reshape(1, -1), inversion, jnp.asarray(make_table()))
    dma = pltpu.SemaphoreType.DMA
    f32, bf16 = jnp.float32, jnp.bfloat16
    return pl.pallas_call(
        kernel,
        out_shape=pltpu.VMEM((16, 16, CYCLES), f32),
        in_specs=[pl.BlockSpec(memory_space=pltpu.HBM)] * 5,
        out_specs=pl.BlockSpec(memory_space=pltpu.VMEM),
        scratch_shapes=[
            pltpu.VMEM((SNAPS, CYCLES, ANGLES), bf16),
            pltpu.VMEM((2 * ORDERS, ANGLES), bf16),
            pltpu.VMEM((LINE * SNAPS, CYCLES), jnp.int32),
            pltpu.VMEM((1, LINE * SNAPS), f32),
            pltpu.VMEM((ORDERS, ORDERS), f32),
            pltpu.VMEM((2, SNAPS * 2 * ORDERS, 128), f32),
            pltpu.VMEM((ORDERS, 2, SNAPS, CYCLES), bf16),
            pltpu.VMEM((GROUPS, 2, LINE, SNAPS, CYCLES), bf16),
            pltpu.VMEM((CYCLES, 128), f32),
            pltpu.VMEM((GROUPS, 8, 128), f32),
            pltpu.VMEM((GROUPS, 1, LINE * SNAPS), f32),
            pltpu.VMEM((CYCLES, CYCLES), f32),
            pltpu.VMEM((ORDERS * 8, 128), f32),
            pltpu.VMEM((HALF, 8, 128), f32),
            dma((4,)),
            dma((SNAPS // CHUNK,)),
            dma, dma, dma,
            dma((GROUPS,)),
            dma, dma, dma,
            dma((SIDE,)),
            dma, dma, dma, dma,
        ],
        compiler_params=pltpu.CompilerParams(
            collective_id=0, has_side_effects=True, vmem_limit_bytes=48 * 2**20
        ),
        name="kam",
    )(*(pltpu.with_memory_space_constraint(value, pltpu.HBM) for value in operands))


def solution(mesh):
    placed = (P(("snap", "ord"), None, None), P("snap", None), P("snap"), P())
    return jax.shard_map(
        on_device, mesh=mesh, in_specs=placed, out_specs=P("ord", "snap", None), check_vma=False
    )
```
